1024 devices in a mesh: hid: 64 (over z, core), row: 16 (over x, y).
Axes of the slice: x: 4, y: 4, z: 32, core: 2. Of those that a mesh axis runs over, the one named last changes fastest.
Arguments:
- inputs: bfloat16 [512, 12288], P('hid', 'row'), may hold values from -6 to 6
- out_grad: bfloat16 [512, 12288], P('hid', 'row'), may hold values from -6 to 6
- pre_act: bfloat16 [512, 24576], P(None, 'hid'), may hold values from -8 to 8
- w_in: bfloat16 [12288, 24576], P('row', 'hid'), may hold values from -0.15625 to 0.15625
- w_out: bfloat16 [24576, 12288], P('hid', 'row'), may hold values from -0.15625 to 0.15625
- pattern_in: int32 [96, 192], P('row', 'hid'), may hold values from 0 to 1, as said below
- pattern_out: int32 [192, 96], P('hid', 'row'), may hold values from 0 to 1, as said below
Outputs:
- in_grad: bfloat16 [512, 12288], P('hid', 'row')
- w_in_grad: bfloat16 [12288, 24576], P('row', 'hid')
- w_out_grad: bfloat16 [24576, 12288], P('hid', 'row')
The draws below stay inside these ranges and needn't reach their ends.
Inputs may be any that keep to these rules, and one draw needn't show every extreme that they name: `pattern_in`: 1 marks a nonzero block; among the blocks that one index of row and one index of hid hold together, at least one is marked. `pattern_out`: 1 marks a nonzero block; among the blocks that one index of hid and one index of row hold together, at least one is marked.
All inputs are finite; a program needn't handle non-finite values.
Results may differ from the reference program's by a relative error of at most 0.0049.
Values may be sent and summed in bfloat16 or wider, within the bound.
No kernel may reach another device: no remote copies, remote signals or barrier semaphores. Data moves between devices by JAX's collectives and lax.ppermute only.
A program may use at most 32 MiB of HBM per device.

```python
import math
import jax
import jax.numpy as jnp

D = 12288
F = 24576
BLOCK = 128
TOKENS = 512
DB = 96
FB = 192
N_HID = 64
N_ROW = 16


def draw_pattern(key, rows, cols, tile_rows, tile_cols):
    draws = jax.random.randint(key, (rows, cols), 0, 8)
    tiles_down = rows // tile_rows
    tiles_across = cols // tile_cols
    pick_row = jax.random.randint(jax.random.fold_in(key, 1), (tiles_down, tiles_across), 0, tile_rows)
    pick_col = jax.random.randint(jax.random.fold_in(key, 2), (tiles_down, tiles_across), 0, tile_cols)
    row_tile = jnp.arange(rows) // tile_rows
    col_tile = jnp.arange(cols) // tile_cols
    row_inner = jnp.arange(rows) % tile_rows
    col_inner = jnp.arange(cols) % tile_cols
    chosen_row = pick_row[row_tile[:, None], col_tile[None, :]]
    chosen_col = pick_col[row_tile[:, None], col_tile[None, :]]
    forced = (row_inner[:, None] == chosen_row) & (col_inner[None, :] == chosen_col)
    return ((draws == 0) | forced).astype(jnp.int32)


def draw_pattern_in(key, part):
    key = jax.random.fold_in(key, 11)
    return draw_pattern(key, DB, FB, DB // N_ROW, FB // N_HID)


def draw_pattern_out(key, part):
    key = jax.random.fold_in(key, 12)
    return draw_pattern(key, FB, DB, FB // N_HID, DB // N_ROW)


def level_of(own_key, dims, shards, smallest, top_value):
    loudness, own = 1.0, jax.random.fold_in(own_key, 6)
    for position, shards_of in shards:
        steps = jnp.exp(jax.random.uniform(jax.random.fold_in(own, position), (shards_of,), jnp.float32, smallest / len(shards), top_value / len(shards)))
        loudness = loudness * jnp.repeat(steps, dims[position] // shards_of).reshape([-1 if axis == position else 1 for axis in range(len(dims))])
    return loudness


def noise(stream_key, dims, width, reach, split=(), dtype=jnp.bfloat16):
    entries = width * jax.random.normal(stream_key, dims, jnp.float32)
    if split:
        entries = entries * level_of(stream_key, dims, split, -0.22, 0.18)
    return jnp.clip(entries, -reach, reach).astype(dtype)


def setup_inputs(seed: int = 0) -> dict:
    arg_keys = jax.random.split(jax.random.key(seed), 8)
    return {
        "inputs": noise(arg_keys[0], (TOKENS, D), 1.0, 6.0, ((0, 64), (1, 16))),
        "out_grad": noise(arg_keys[1], (TOKENS, D), 1.0, 6.0, ((0, 64), (1, 16))),
        "pre_act": noise(arg_keys[2], (TOKENS, F), 1.5, 8.0, ((1, 64),)),
        "w_in": noise(arg_keys[3], (D, F), (D // 8) ** -0.5, 0.15625, ((0, 16), (1, 64))),
        "w_out": noise(arg_keys[4], (F, D), (D // 8) ** -0.5, 0.15625, ((0, 64), (1, 16))),
        "pattern_in": draw_pattern_in(jax.random.fold_in(arg_keys[7], 71), 0),
        "pattern_out": draw_pattern_out(jax.random.fold_in(arg_keys[7], 71), 0),
    }


def widen(pattern, block):
    rows, cols = pattern.shape
    wide = jnp.broadcast_to(pattern.astype(jnp.bfloat16)[:, None, :, None], (rows, block, cols, block))
    return wide.reshape(rows * block, cols * block)

def gelu_parts(pre_act):
    values = pre_act.astype(jnp.float32)
    return jax.jvp(lambda v: jax.nn.gelu(v, approximate=True), (values,), (jnp.ones_like(values),))

def reference(inputs, out_grad, pre_act, w_in, w_out, pattern_in, pattern_out):
    mask_in = widen(pattern_in, BLOCK)
    mask_out = widen(pattern_out, BLOCK)
    w_in_eff = w_in * mask_in
    w_out_eff = w_out * mask_out
    value, slope = gelu_parts(pre_act)
    act = value.astype(jnp.bfloat16)
    act_grad = jnp.dot(out_grad, w_out_eff.T, preferred_element_type=jnp.float32)
    delta = (act_grad * slope).astype(jnp.bfloat16)
    in_grad = jnp.dot(delta, w_in_eff.T, preferred_element_type=jnp.float32).astype(jnp.bfloat16)
    scale = 1.0 / math.sqrt(TOKENS)
    w_in_grad = jnp.dot(inputs.T, delta, preferred_element_type=jnp.float32) * scale
    w_in_grad = (w_in_grad * mask_in.astype(jnp.float32)).astype(jnp.bfloat16)
    w_out_grad = jnp.dot(act.T, out_grad, preferred_element_type=jnp.float32) * scale
    w_out_grad = (w_out_grad * mask_out.astype(jnp.float32)).astype(jnp.bfloat16)
    return (in_grad, w_in_grad, w_out_grad)
```

```python
import math

import jax
import jax.numpy as jnp
from jax import lax
from jax.sharding import PartitionSpec as P

BLOCK = 128
NEAR = 4


def widen(pattern, block):
    rows, cols = pattern.shape
    wide = jnp.broadcast_to(
        pattern.astype(jnp.bfloat16)[:, None, :, None], (rows, block, cols, block)
    )
    return wide.reshape(rows * block, cols * block)


def gelu_parts(pre_act):
    values = pre_act.astype(jnp.float32)
    return jax.jvp(lambda v: jax.nn.gelu(v, approximate=True), (values,), (jnp.ones_like(values),))


def groups(n_hid):
    far = n_hid // 2 // NEAR
    at = lambda k, n, c: 2 * (NEAR * k + n) + c
    return (
        [[at(k, n, c) for k in range(far)] for n in range(NEAR) for c in range(2)],
        [[at(k, n, c) for n in range(NEAR)] for k in range(far) for c in range(2)],
        [[at(k, n, c) for c in range(2)] for k in range(far) for n in range(NEAR)],
    )


def swap(x, axis, within=None):
    return lax.all_to_all(x, axis, 0, 0, tiled=True, axis_index_groups=within)


def spread(x, axis, count, within=None):
    many = jnp.broadcast_to(x[None], (count,) + x.shape).reshape((count * x.shape[0],) + x.shape[1:])
    return swap(many, axis, within)


def shards(n_hid, n_row, inputs, out_grad, pre_act, w_in, w_out, pattern_in, pattern_out):
    far_groups, near_groups, pairs = groups(n_hid)
    far = n_hid // 2 // NEAR
    tokens, width = pre_act.shape
    own = out_grad.shape[0]
    core = lax.axis_index("hid") % 2

    def gather(x):
        x = spread(x, "hid", far, far_groups)
        x = spread(x, "hid", NEAR, near_groups)
        return lax.all_gather(x, "hid", axis=0, tiled=True, axis_index_groups=pairs)

    mask_in = widen(pattern_in, BLOCK)
    mask_out = widen(pattern_out, BLOCK)
    w_in_eff = w_in * mask_in
    w_out_eff = w_out * mask_out
    ordered = pre_act.reshape(far, NEAR, 2, own, width).transpose(2, 1, 0, 3, 4).reshape(tokens, width)
    value, slope = gelu_parts(ordered)
    act = value.astype(jnp.bfloat16)

    panel = gather(out_grad)
    partial = lax.dot_general(
        panel, w_out_eff, (((1,), (1,)), ((), ())), preferred_element_type=jnp.float32
    )
    share = tokens // n_row
    summed = jnp.sum(swap(partial, "row").reshape(n_row, share, width), axis=0)
    slope_share = lax.dynamic_slice_in_dim(slope, lax.axis_index("row") * share, share, 0)
    delta = spread((summed * slope_share).astype(jnp.bfloat16), "row", n_row)

    back = lax.dot_general(
        delta, w_in_eff, (((1,), (1,)), ((), ())), preferred_element_type=jnp.float32
    )
    features = back.shape[1]
    back = back.reshape(2, tokens // 2, features)
    mine = lax.dynamic_index_in_dim(back, core, 0, keepdims=False)
    other = lax.dynamic_index_in_dim(back, 1 - core, 0, keepdims=False)
    got = lax.ppermute(other, "hid", [(i, i ^ 1) for i in range(n_hid)])
    back = (mine + got).astype(jnp.bfloat16)
    back = swap(back, "hid", near_groups).astype(jnp.float32)
    back = jnp.sum(back.reshape(NEAR, far * own, features), axis=0).astype(jnp.bfloat16)
    back = swap(back, "hid", far_groups).astype(jnp.float32)
    in_grad = jnp.sum(back.reshape(far, own, features), axis=0).astype(jnp.bfloat16)

    in_weight = lax.dot_general(
        gather(inputs), delta, (((0,), (0,)), ((), ())), preferred_element_type=jnp.float32
    )
    out_weight = lax.dot_general(
        act, panel, (((0,), (0,)), ((), ())), preferred_element_type=jnp.float32
    )
    scale = 1.0 / math.sqrt(tokens)
    w_in_grad = (in_weight * scale * mask_in.astype(jnp.float32)).astype(jnp.bfloat16)
    w_out_grad = (out_weight * scale * mask_out.astype(jnp.float32)).astype(jnp.bfloat16)
    return (in_grad, w_in_grad, w_out_grad)


def solution(mesh):
    placed = (
        P("hid", "row"),
        P("hid", "row"),
        P(None, "hid"),
        P("row", "hid"),
        P("hid", "row"),
        P("row", "hid"),
        P("hid", "row"),
    )
    return jax.shard_map(
        lambda *blocks: shards(mesh.shape["hid"], mesh.shape["row"], *blocks),
        mesh=mesh,
        in_specs=placed,
        out_specs=(P("hid", "row"), P("row", "hid"), P("hid", "row")),
        check_vma=False,
    )
```

```python
import math

import jax
import jax.numpy as jnp
from jax import lax
from jax.experimental import pallas as pl
from jax.experimental.pallas import tpu as pltpu
from jax.sharding import PartitionSpec as P

BLOCK = 128
NEAR = 4
CONTRACT_LAST = (((1,), (1,)), ((), ()))
CONTRACT_FIRST = (((0,), (0,)), ((), ()))


def widen(pattern, block):
    rows, cols = pattern.shape
    wide = jnp.broadcast_to(
        pattern.astype(jnp.bfloat16)[:, None, :, None], (rows, block, cols, block)
    )
    return wide.reshape(rows * block, cols * block)


def gelu_parts(pre_act):
    values = pre_act.astype(jnp.float32)
    return jax.jvp(lambda v: jax.nn.gelu(v, approximate=True), (values,), (jnp.ones_like(values),))


def groups(n_hid):
    far = n_hid // 2 // NEAR
    at = lambda k, n, c: 2 * (NEAR * k + n) + c
    return (
        [[at(k, n, c) for k in range(far)] for n in range(NEAR) for c in range(2)],
        [[at(k, n, c) for n in range(NEAR)] for k in range(far) for c in range(2)],
    )


def swap(x, axis, within=None):
    return lax.all_to_all(x, axis, 0, 0, axis_index_groups=within, tiled=True)


def local(body, out_shape, flops, *args):
    size = sum(a.size * a.dtype.itemsize for a in (*args, out_shape))
    return pl.pallas_call(
        body,
        out_shape=out_shape,
        in_specs=[pl.BlockSpec(memory_space=pltpu.VMEM)] * len(args),
        out_specs=pl.BlockSpec(memory_space=pltpu.VMEM),
        compiler_params=pltpu.CompilerParams(vmem_limit_bytes=24 * 2**20),
        cost_estimate=pl.CostEstimate(flops=flops, bytes_accessed=size, transcendentals=0),
    )(*args)


def act_grad_body(rows_ref, own_ref, got_ref, out_ref):
    width, features = own_ref.shape
    rows = rows_ref[:, :features]
    out_ref[:, :width] = lax.dot_general(
        rows, own_ref[...], CONTRACT_LAST, preferred_element_type=jnp.float32
    )
    out_ref[:, width:] = lax.dot_general(
        rows, got_ref[...], CONTRACT_LAST, preferred_element_type=jnp.float32
    )


def delta_body(parts_ref, slope_ref, out_ref):
    total = parts_ref[0]
    for part in range(1, parts_ref.shape[0]):
        total = total + parts_ref[part]
    delta = (total * slope_ref[...]).astype(out_ref.dtype)
    for copy in range(out_ref.shape[0]):
        out_ref[copy] = delta


def in_grad_body(delta_ref, own_ref, got_ref, out_ref):
    width = own_ref.shape[1]
    total = lax.dot_general(
        delta_ref[:, :width], own_ref[...], CONTRACT_LAST, preferred_element_type=jnp.float32
    )
    total = total + lax.dot_general(
        delta_ref[:, width:], got_ref[...], CONTRACT_LAST, preferred_element_type=jnp.float32
    )
    out_ref[...] = total.astype(out_ref.dtype)


def sum_body(parts_ref, out_ref):
    total = parts_ref[0].astype(jnp.float32)
    for part in range(1, parts_ref.shape[0]):
        total = total + parts_ref[part].astype(jnp.float32)
    out_ref[...] = total.astype(out_ref.dtype)


def over_tokens(left, right):
    return lax.dot_general(left, right, CONTRACT_FIRST, preferred_element_type=jnp.float32)


def w_in_grad_body(scale, rows_ref, rows_got_ref, delta_ref, delta_got_ref, mask_ref, out_ref):
    features = out_ref.shape[0]
    grad = over_tokens(rows_ref[:, features:], delta_ref[...])
    grad = grad + over_tokens(rows_got_ref[:, features:], delta_got_ref[...])
    out_ref[...] = (grad * scale * mask_ref[...].astype(jnp.float32)).astype(out_ref.dtype)


def w_out_grad_body(scale, act_ref, act_other_ref, rows_ref, rows_got_ref, mask_ref, out_ref):
    features = out_ref.shape[1]
    grad = over_tokens(act_ref[...], rows_ref[:, :features])
    grad = grad + over_tokens(act_other_ref[...], rows_got_ref[:, :features])
    out_ref[...] = (grad * scale * mask_ref[...].astype(jnp.float32)).astype(out_ref.dtype)


def shards(n_hid, n_row, inputs, out_grad, pre_act, w_in, w_out, pattern_in, pattern_out):
    far_groups, near_groups = groups(n_hid)
    far = n_hid // 2 // NEAR
    tokens, width = pre_act.shape
    own, features = out_grad.shape
    half = tokens // 2
    share = half // n_row
    runs = share // own
    core = lax.axis_index("hid") % 2
    row = lax.axis_index("row")
    struct = jax.ShapeDtypeStruct

    other = 1 - core

    def partner(x):
        return lax.ppermute(x, "hid", [(i, i ^ 1) for i in range(n_hid)])

    mask_in = widen(pattern_in, BLOCK)
    mask_out = widen(pattern_out, BLOCK)
    w_in_eff = w_in * mask_in
    w_out_eff = w_out * mask_out
    w_in_got = partner(w_in_eff)
    w_out_got = partner(w_out_eff)
    placed = pre_act.reshape(far, NEAR, 2, own, width)
    first = (row % (far // runs)) * runs
    mine = lax.dynamic_slice_in_dim(placed, first, runs, 0)
    mine = lax.dynamic_index_in_dim(mine, row // (far // runs), 1, keepdims=False)
    pre_own = lax.dynamic_index_in_dim(mine, core, 1, keepdims=False).reshape(share, width)
    pre_other = lax.dynamic_index_in_dim(mine, other, 1, keepdims=False).reshape(share, width)
    _, slope = gelu_parts(jnp.concatenate([pre_own, partner(pre_other)], axis=1))

    both = jnp.concatenate([out_grad, inputs], axis=1)
    rows = swap(jnp.broadcast_to(both[None], (far, own, 2 * features)), "hid", far_groups)
    rows, w_out_got, w_in_got, slope, w_in_eff, w_out_eff = lax.optimization_barrier(
        (rows, w_out_got, w_in_got, slope, w_in_eff, w_out_eff)
    )
    rows = rows.reshape(1, far * own, 2 * features)
    rows = swap(jnp.broadcast_to(rows, (NEAR, far * own, 2 * features)), "hid", near_groups)
    rows = rows.reshape(half, 2 * features)

    partial = local(
        act_grad_body,
        struct((half, 2 * width), jnp.float32),
        4 * half * features * width,
        rows,
        w_out_eff,
        w_out_got,
    )
    parts = swap(partial.reshape(n_row, share, 2 * width), "row")
    copies = local(
        delta_body,
        struct((n_row, share, 2 * width), jnp.bfloat16),
        n_row * share * width,
        parts,
        slope,
    )
    delta = swap(copies, "row").reshape(half, 2 * width)

    back = local(
        in_grad_body,
        struct((half, features), jnp.bfloat16),
        4 * half * features * width,
        delta,
        w_in_eff,
        w_in_got,
    )
    back = swap(back.reshape(NEAR, far * own, features), "hid", near_groups)
    back = local(sum_body, struct((far * own, features), jnp.bfloat16), back.size, back)
    back = swap(back.reshape(far, own, features), "hid", far_groups)
    in_grad = local(sum_body, struct((own, features), jnp.bfloat16), back.size, back)

    scale = 1.0 / math.sqrt(tokens)
    rows_got = partner(rows)
    w_in_grad = local(
        lambda *refs: w_in_grad_body(scale, *refs),
        struct((features, width), jnp.bfloat16),
        2 * tokens * features * width,
        rows,
        rows_got,
        delta[:, :width],
        partner(delta[:, width:]),
        mask_in,
    )
    value, _ = gelu_parts(placed.transpose(2, 1, 0, 3, 4).reshape(2, half, width))
    act = value.astype(jnp.bfloat16)
    w_out_grad = local(
        lambda *refs: w_out_grad_body(scale, *refs),
        struct((width, features), jnp.bfloat16),
        2 * tokens * features * width,
        lax.dynamic_index_in_dim(act, core, 0, keepdims=False),
        lax.dynamic_index_in_dim(act, other, 0, keepdims=False),
        rows,
        rows_got,
        mask_out,
    )
    return (in_grad, w_in_grad, w_out_grad)


def solution(mesh):
    placed = (
        P("hid", "row"),
        P("hid", "row"),
        P(None, "hid"),
        P("row", "hid"),
        P("hid", "row"),
        P("row", "hid"),
        P("hid", "row"),
    )
    return jax.shard_map(
        lambda *blocks: shards(mesh.shape["hid"], mesh.shape["row"], *blocks),
        mesh=mesh,
        in_specs=placed,
        out_specs=(P("hid", "row"), P("row", "hid"), P("hid", "row")),
        check_vma=False,
    )
```

```python
import math

import jax
import jax.numpy as jnp
from jax import lax
from jax.experimental import pallas as pl
from jax.experimental.pallas import tpu as pltpu
from jax.sharding import PartitionSpec as P

BLOCK = 128
NEAR = 4
CONTRACT_LAST = (((1,), (1,)), ((), ()))
CONTRACT_FIRST = (((0,), (0,)), ((), ()))


def widen(pattern, block):
    rows, cols = pattern.shape
    wide = jnp.broadcast_to(
        pattern.astype(jnp.bfloat16)[:, None, :, None], (rows, block, cols, block)
    )
    return wide.reshape(rows * block, cols * block)


def gelu_parts(pre_act):
    values = pre_act.astype(jnp.float32)
    return jax.jvp(lambda v: jax.nn.gelu(v, approximate=True), (values,), (jnp.ones_like(values),))


def groups(n_hid):
    far = n_hid // 2 // NEAR
    at = lambda k, n, c: 2 * (NEAR * k + n) + c
    return (
        [[at(k, n, c) for k in range(far)] for n in range(NEAR) for c in range(2)],
        [[at(k, n, c) for n in range(NEAR)] for k in range(far) for c in range(2)],
    )


def swap(x, axis, within=None):
    return lax.all_to_all(x, axis, 0, 0, axis_index_groups=within, tiled=True)


def local(body, out_shape, flops, *args):
    size = sum(a.size * a.dtype.itemsize for a in (*args, out_shape))
    return pl.pallas_call(
        body,
        out_shape=out_shape,
        in_specs=[pl.BlockSpec(memory_space=pltpu.VMEM)] * len(args),
        out_specs=pl.BlockSpec(memory_space=pltpu.VMEM),
        compiler_params=pltpu.CompilerParams(vmem_limit_bytes=24 * 2**20),
        cost_estimate=pl.CostEstimate(flops=flops, bytes_accessed=size, transcendentals=0),
    )(*args)


def act_grad_body(rows_ref, own_ref, got_ref, out_ref):
    width = own_ref.shape[0]
    rows = rows_ref[...]
    out_ref[:, :width] = lax.dot_general(
        rows, own_ref[...], CONTRACT_LAST, preferred_element_type=jnp.float32
    )
    out_ref[:, width:] = lax.dot_general(
        rows, got_ref[...], CONTRACT_LAST, preferred_element_type=jnp.float32
    )


def delta_body(parts_ref, slope_ref, out_ref):
    total = parts_ref[0]
    for part in range(1, parts_ref.shape[0]):
        total = total + parts_ref[part]
    delta = (total * slope_ref[...]).astype(out_ref.dtype)
    for copy in range(out_ref.shape[0]):
        out_ref[copy] = delta


def in_grad_body(delta_ref, own_ref, got_ref, out_ref):
    width = own_ref.shape[1]
    total = lax.dot_general(
        delta_ref[:, :width], own_ref[...], CONTRACT_LAST, preferred_element_type=jnp.float32
    )
    total = total + lax.dot_general(
        delta_ref[:, width:], got_ref[...], CONTRACT_LAST, preferred_element_type=jnp.float32
    )
    out_ref[...] = total.astype(out_ref.dtype)


def sum_body(parts_ref, out_ref):
    total = parts_ref[0].astype(jnp.float32)
    for part in range(1, parts_ref.shape[0]):
        total = total + parts_ref[part].astype(jnp.float32)
    out_ref[...] = total.astype(out_ref.dtype)


def over_tokens(left, right):
    return lax.dot_general(left, right, CONTRACT_FIRST, preferred_element_type=jnp.float32)


def w_in_grad_body(scale, panel_ref, delta_ref, mask_ref, out_ref):
    grad = over_tokens(panel_ref[...].astype(jnp.bfloat16), delta_ref[...])
    out_ref[...] = (grad * scale * mask_ref[...].astype(jnp.float32)).astype(out_ref.dtype)


def w_out_grad_body(scale, act_ref, act_other_ref, rows_ref, rows_got_ref, mask_ref, out_ref):
    grad = over_tokens(act_ref[...], rows_ref[...])
    grad = grad + over_tokens(act_other_ref[...], rows_got_ref[...])
    out_ref[...] = (grad * scale * mask_ref[...].astype(jnp.float32)).astype(out_ref.dtype)


def partner(x):
    count = lax.axis_size("hid")
    return lax.ppermute(x, "hid", [(i, i ^ 1) for i in range(count)])


def chain(n_hid, n_row, out_grad, pre_act, w_in, w_out, pattern_in, pattern_out):
    far_groups, near_groups = groups(n_hid)
    far = n_hid // 2 // NEAR
    tokens, width = pre_act.shape
    own, features = out_grad.shape
    half = tokens // 2
    share = half // n_row
    runs = share // own
    core = lax.axis_index("hid") % 2
    row = lax.axis_index("row")
    struct = jax.ShapeDtypeStruct

    w_in_eff = w_in * widen(pattern_in, BLOCK)
    w_out_eff = w_out * widen(pattern_out, BLOCK)
    w_in_got = partner(w_in_eff)
    w_out_got = partner(w_out_eff)
    placed = pre_act.reshape(far, NEAR, 2, own, width)
    first = (row % (far // runs)) * runs
    mine = lax.dynamic_slice_in_dim(placed, first, runs, 0)
    mine = lax.dynamic_index_in_dim(mine, row // (far // runs), 1, keepdims=False)
    pre_own = lax.dynamic_index_in_dim(mine, core, 1, keepdims=False).reshape(share, width)
    pre_other = lax.dynamic_index_in_dim(mine, 1 - core, 1, keepdims=False).reshape(share, width)
    _, slope = gelu_parts(jnp.concatenate([pre_own, partner(pre_other)], axis=1))

    rows = swap(jnp.broadcast_to(out_grad[None], (far, own, features)), "hid", far_groups)
    rows, w_out_got, w_in_got, slope, w_in_eff, w_out_eff = lax.optimization_barrier(
        (rows, w_out_got, w_in_got, slope, w_in_eff, w_out_eff)
    )
    rows = rows.reshape(1, far * own, features)
    rows = swap(jnp.broadcast_to(rows, (NEAR, far * own, features)), "hid", near_groups)
    rows = rows.reshape(half, features)

    partial = local(
        act_grad_body,
        struct((half, 2 * width), jnp.float32),
        4 * half * features * width,
        rows,
        w_out_eff,
        w_out_got,
    )
    parts = swap(partial.reshape(n_row, share, 2 * width), "row")
    copies = local(
        delta_body,
        struct((n_row, share, 2 * width), jnp.bfloat16),
        n_row * share * width,
        parts,
        slope,
    )
    delta = swap(copies, "row").reshape(half, 2 * width)

    back = local(
        in_grad_body,
        struct((half, features), jnp.bfloat16),
        4 * half * features * width,
        delta,
        w_in_eff,
        w_in_got,
    )
    back = swap(back.reshape(NEAR, far * own, features), "hid", near_groups)
    back = local(sum_body, struct((far * own, features), jnp.bfloat16), back.size, back)
    return back, delta, rows


def shards(n_hid, n_row, inputs, out_grad, pre_act, w_in, w_out, pattern_in, pattern_out):
    far_groups, _ = groups(n_hid)
    far = n_hid // 2 // NEAR
    tokens, width = pre_act.shape
    own, features = out_grad.shape
    half = tokens // 2
    core = lax.axis_index("hid") % 2
    struct = jax.ShapeDtypeStruct

    mask_in = widen(pattern_in, BLOCK)
    mask_out = widen(pattern_out, BLOCK)
    in_panel = lax.all_gather(inputs.astype(jnp.float32), "hid", axis=0, tiled=True)
    back, delta, rows = lax.cond(
        pattern_in[0, 0] >= 0,
        lambda *args: chain(n_hid, n_row, *args),
        lambda *args: (
            jnp.zeros((far * own, features), jnp.bfloat16),
            jnp.zeros((half, 2 * width), jnp.bfloat16),
            jnp.zeros((half, features), jnp.bfloat16),
        ),
        out_grad,
        pre_act,
        w_in,
        w_out,
        pattern_in,
        pattern_out,
    )
    back = swap(back.reshape(far, own, features), "hid", far_groups)
    in_grad = local(sum_body, struct((own, features), jnp.bfloat16), back.size, back)

    scale = 1.0 / math.sqrt(tokens)
    delta_own, delta_got = delta[:, :width], partner(delta[:, width:])
    by_core = lax.dynamic_slice_in_dim(
        jnp.concatenate([delta_own, delta_got, delta_own], axis=0), core * half, tokens, 0
    )
    by_token = by_core.reshape(2, NEAR, far, own, width).transpose(2, 1, 0, 3, 4)
    w_in_grad = local(
        lambda *refs: w_in_grad_body(scale, *refs),
        struct((features, width), jnp.bfloat16),
        2 * tokens * features * width,
        in_panel,
        by_token.reshape(tokens, width),
        mask_in,
    )
    value, _ = gelu_parts(pre_act)
    act = value.astype(jnp.bfloat16).reshape(far, NEAR, 2, own, width)
    act = act.transpose(2, 1, 0, 3, 4).reshape(2, half, width)
    w_out_grad = local(
        lambda *refs: w_out_grad_body(scale, *refs),
        struct((width, features), jnp.bfloat16),
        2 * tokens * features * width,
        lax.dynamic_index_in_dim(act, core, 0, keepdims=False),
        lax.dynamic_index_in_dim(act, 1 - core, 0, keepdims=False),
        rows,
        partner(rows),
        mask_out,
    )
    return (in_grad, w_in_grad, w_out_grad)


def solution(mesh):
    placed = (
        P("hid", "row"),
        P("hid", "row"),
        P(None, "hid"),
        P("row", "hid"),
        P("hid", "row"),
        P("row", "hid"),
        P("hid", "row"),
    )
    return jax.shard_map(
        lambda *blocks: shards(mesh.shape["hid"], mesh.shape["row"], *blocks),
        mesh=mesh,
        in_specs=placed,
        out_specs=(P("hid", "row"), P("row", "hid"), P("hid", "row")),
        check_vma=False,
    )
```

```python
import math

import jax
import jax.numpy as jnp
from jax import lax
from jax.experimental import pallas as pl
from jax.experimental.pallas import tpu as pltpu
from jax.sharding import PartitionSpec as P

BLOCK = 128
NEAR = 4
CONTRACT_LAST = (((1,), (1,)), ((), ()))
CONTRACT_FIRST = (((0,), (0,)), ((), ()))


def widen(pattern, block):
    rows, cols = pattern.shape
    wide = jnp.broadcast_to(
        pattern.astype(jnp.bfloat16)[:, None, :, None], (rows, block, cols, block)
    )
    return wide.reshape(rows * block, cols * block)


def gelu_parts(pre_act):
    values = pre_act.astype(jnp.float32)
    return jax.jvp(lambda v: jax.nn.gelu(v, approximate=True), (values,), (jnp.ones_like(values),))


def groups(n_hid):
    far = n_hid // 2 // NEAR
    at = lambda k, n, c: 2 * (NEAR * k + n) + c
    return (
        [[at(k, n, c) for k in range(far)] for n in range(NEAR) for c in range(2)],
        [[at(k, n, c) for n in range(NEAR)] for k in range(far) for c in range(2)],
    )


def swap(x, axis, within=None):
    return lax.all_to_all(x, axis, 0, 0, axis_index_groups=within, tiled=True)


def local(body, out_shape, flops, *args):
    size = sum(a.size * a.dtype.itemsize for a in (*args, out_shape))
    return pl.pallas_call(
        body,
        out_shape=out_shape,
        in_specs=[pl.BlockSpec(memory_space=pltpu.VMEM)] * len(args),
        out_specs=pl.BlockSpec(memory_space=pltpu.VMEM),
        compiler_params=pltpu.CompilerParams(vmem_limit_bytes=24 * 2**20),
        cost_estimate=pl.CostEstimate(flops=flops, bytes_accessed=size, transcendentals=0),
    )(*args)


def act_grad_body(rows_ref, own_ref, got_ref, out_ref):
    width = own_ref.shape[0]
    rows = rows_ref[...]
    out_ref[:, :width] = lax.dot_general(
        rows, own_ref[...], CONTRACT_LAST, preferred_element_type=jnp.float32
    )
    out_ref[:, width:] = lax.dot_general(
        rows, got_ref[...], CONTRACT_LAST, preferred_element_type=jnp.float32
    )


def spread_body(left_ref, right_ref, out_ref):
    width = left_ref.shape[1]
    for copy in range(out_ref.shape[0]):
        out_ref[copy, :, :width] = left_ref[...]
        out_ref[copy, :, width:] = right_ref[...]


def place_body(spots_ref, *refs):
    *blocks, out_ref = refs
    for block, block_ref in enumerate(blocks):
        count = block_ref.shape[0]
        out_ref[pl.ds(pl.multiple_of(spots_ref[block] * count, count), count), :] = block_ref[...]


def delta_body(parts_ref, slope_ref, out_ref):
    total = parts_ref[0]
    for part in range(1, parts_ref.shape[0]):
        total = total + parts_ref[part]
    delta = (total * slope_ref[...]).astype(out_ref.dtype)
    for copy in range(out_ref.shape[0]):
        out_ref[copy] = delta


def in_grad_body(delta_ref, own_ref, got_ref, out_ref):
    width = own_ref.shape[1]
    total = lax.dot_general(
        delta_ref[:, :width], own_ref[...], CONTRACT_LAST, preferred_element_type=jnp.float32
    )
    total = total + lax.dot_general(
        delta_ref[:, width:], got_ref[...], CONTRACT_LAST, preferred_element_type=jnp.float32
    )
    out_ref[...] = total.astype(out_ref.dtype)


def sum_body(parts_ref, out_ref):
    total = parts_ref[0].astype(jnp.float32)
    for part in range(1, parts_ref.shape[0]):
        total = total + parts_ref[part].astype(jnp.float32)
    out_ref[...] = total.astype(out_ref.dtype)


def over_tokens(left, right):
    return lax.dot_general(left, right, CONTRACT_FIRST, preferred_element_type=jnp.float32)


def w_in_grad_body(scale, rows_ref, rows_got_ref, delta_ref, delta_got_ref, mask_ref, out_ref):
    grad = over_tokens(rows_ref[...], delta_ref[...])
    grad = grad + over_tokens(rows_got_ref[...], delta_got_ref[...])
    out_ref[...] = (grad * scale * mask_ref[...].astype(jnp.float32)).astype(out_ref.dtype)


def w_out_grad_body(scale, act_ref, act_other_ref, rows_ref, rows_got_ref, mask_ref, out_ref):
    grad = over_tokens(act_ref[...], rows_ref[...])
    grad = grad + over_tokens(act_other_ref[...], rows_got_ref[...])
    out_ref[...] = (grad * scale * mask_ref[...].astype(jnp.float32)).astype(out_ref.dtype)


def shards(n_hid, n_row, inputs, out_grad, pre_act, w_in, w_out, pattern_in, pattern_out):
    far_groups, near_groups = groups(n_hid)
    far = n_hid // 2 // NEAR
    tokens, width = pre_act.shape
    own, features = out_grad.shape
    half = tokens // 2
    share = half // n_row
    runs = share // own
    core = lax.axis_index("hid") % 2
    row = lax.axis_index("row")
    struct = jax.ShapeDtypeStruct

    other = 1 - core

    def partner(x):
        return lax.ppermute(x, "hid", [(i, i ^ 1) for i in range(n_hid)])

    mask_in = widen(pattern_in, BLOCK)
    mask_out = widen(pattern_out, BLOCK)
    w_in_eff = w_in * mask_in
    w_out_eff = w_out * mask_out
    w_in_got = partner(w_in_eff)
    w_out_got = partner(w_out_eff)
    placed = pre_act.reshape(far, NEAR, 2, own, width)
    first = (row % (far // runs)) * runs
    mine = lax.dynamic_slice_in_dim(placed, first, runs, 0)
    mine = lax.dynamic_index_in_dim(mine, row // (far // runs), 1, keepdims=False)
    pre_own = lax.dynamic_index_in_dim(mine, core, 1, keepdims=False).reshape(share, width)
    pre_other = lax.dynamic_index_in_dim(mine, other, 1, keepdims=False).reshape(share, width)
    _, slope = gelu_parts(jnp.concatenate([pre_own, partner(pre_other)], axis=1))

    both = local(spread_body, struct((far, own, 2 * features), jnp.bfloat16), 0, out_grad, inputs)
    rows = swap(both, "hid", far_groups)
    rows, w_out_got, w_in_got, slope, w_in_eff, w_out_eff = lax.optimization_barrier(
        (rows, w_out_got, w_in_got, slope, w_in_eff, w_out_eff)
    )
    rows = rows.reshape(far * own, 2 * features)
    in_block = rows[:, features:]
    rows = jnp.broadcast_to(rows[None, :, :features], (NEAR, far * own, features))
    rows = swap(rows, "hid", near_groups).reshape(half, features)

    n = lax.axis_index("hid") // 2 % NEAR
    spots = jnp.stack([(n + NEAR - step) % NEAR for step in range(NEAR)]).astype(jnp.int32)
    in_blocks = [in_block]
    for step in range(1, NEAR):
        pairs = [
            (i, i - 2 * (i // 2 % NEAR) + 2 * ((i // 2 + step) % NEAR)) for i in range(n_hid)
        ]
        in_blocks.append(lax.ppermute(in_block, "hid", pairs))
    partial = local(
        act_grad_body,
        struct((half, 2 * width), jnp.float32),
        4 * half * features * width,
        rows,
        w_out_eff,
        w_out_got,
    )
    parts = swap(partial.reshape(n_row, share, 2 * width), "row")
    parts, *in_blocks[1:3] = lax.optimization_barrier((parts, *in_blocks[1:3]))
    copies = local(
        delta_body,
        struct((n_row, share, 2 * width), jnp.bfloat16),
        n_row * share * width,
        parts,
        slope,
    )
    delta = swap(copies, "row").reshape(half, 2 * width)
    delta, *in_blocks[3:] = lax.optimization_barrier((delta, *in_blocks[3:]))

    in_rows = pl.pallas_call(
        place_body,
        out_shape=struct((half, features), jnp.bfloat16),
        in_specs=[pl.BlockSpec(memory_space=pltpu.SMEM)]
        + [pl.BlockSpec(memory_space=pltpu.VMEM)] * NEAR,
        out_specs=pl.BlockSpec(memory_space=pltpu.VMEM),
        compiler_params=pltpu.CompilerParams(vmem_limit_bytes=24 * 2**20),
        cost_estimate=pl.CostEstimate(
            flops=0, bytes_accessed=4 * half * features, transcendentals=0
        ),
    )(spots, *in_blocks)

    back = local(
        in_grad_body,
        struct((half, features), jnp.bfloat16),
        4 * half * features * width,
        delta,
        w_in_eff,
        w_in_got,
    )
    back = swap(back.reshape(NEAR, far * own, features), "hid", near_groups)
    back = local(sum_body, struct((far * own, features), jnp.bfloat16), back.size, back)
    back = swap(back.reshape(far, own, features), "hid", far_groups)
    in_grad = local(sum_body, struct((own, features), jnp.bfloat16), back.size, back)

    scale = 1.0 / math.sqrt(tokens)
    w_in_grad = local(
        lambda *refs: w_in_grad_body(scale, *refs),
        struct((features, width), jnp.bfloat16),
        2 * tokens * features * width,
        in_rows,
        partner(in_rows),
        delta[:, :width],
        partner(delta[:, width:]),
        mask_in,
    )
    value, _ = gelu_parts(placed.transpose(2, 1, 0, 3, 4).reshape(2, half, width))
    act = value.astype(jnp.bfloat16)
    w_out_grad = local(
        lambda *refs: w_out_grad_body(scale, *refs),
        struct((width, features), jnp.bfloat16),
        2 * tokens * features * width,
        lax.dynamic_index_in_dim(act, core, 0, keepdims=False),
        lax.dynamic_index_in_dim(act, other, 0, keepdims=False),
        rows,
        partner(rows),
        mask_out,
    )
    return (in_grad, w_in_grad, w_out_grad)


def solution(mesh):
    placed = (
        P("hid", "row"),
        P("hid", "row"),
        P(None, "hid"),
        P("row", "hid"),
        P("hid", "row"),
        P("row", "hid"),
        P("hid", "row"),
    )
    return jax.shard_map(
        lambda *blocks: shards(mesh.shape["hid"], mesh.shape["row"], *blocks),
        mesh=mesh,
        in_specs=placed,
        out_specs=(P("hid", "row"), P("row", "hid"), P("hid", "row")),
        check_vma=False,
    )
```

```python
import math

import jax
import jax.numpy as jnp
from jax import lax
from jax.experimental import pallas as pl
from jax.experimental.pallas import tpu as pltpu
from jax.sharding import PartitionSpec as P

BLOCK = 128
NEAR = 4
CONTRACT_LAST = (((1,), (1,)), ((), ()))
CONTRACT_FIRST = (((0,), (0,)), ((), ()))


def widen(pattern, block):
    rows, cols = pattern.shape
    wide = jnp.broadcast_to(
        pattern.astype(jnp.bfloat16)[:, None, :, None], (rows, block, cols, block)
    )
    return wide.reshape(rows * block, cols * block)


def gelu_parts(pre_act):
    values = pre_act.astype(jnp.float32)
    return jax.jvp(lambda v: jax.nn.gelu(v, approximate=True), (values,), (jnp.ones_like(values),))


def groups(n_hid):
    far = n_hid // 2 // NEAR
    at = lambda k, n, c: 2 * (NEAR * k + n) + c
    return (
        [[at(k, n, c) for k in range(far)] for n in range(NEAR) for c in range(2)],
        [[at(k, n, c) for n in range(NEAR)] for k in range(far) for c in range(2)],
    )


def swap(x, axis, within=None):
    return lax.all_to_all(x, axis, 0, 0, axis_index_groups=within, tiled=True)


def local(body, out_shape, flops, *args):
    size = sum(a.size * a.dtype.itemsize for a in (*args, out_shape))
    return pl.pallas_call(
        body,
        out_shape=out_shape,
        in_specs=[pl.BlockSpec(memory_space=pltpu.VMEM)] * len(args),
        out_specs=pl.BlockSpec(memory_space=pltpu.VMEM),
        compiler_params=pltpu.CompilerParams(vmem_limit_bytes=24 * 2**20),
        cost_estimate=pl.CostEstimate(flops=flops, bytes_accessed=size, transcendentals=0),
    )(*args)


def act_grad_body(rows_ref, own_ref, got_ref, out_ref):
    width = own_ref.shape[0]
    rows = rows_ref[...]
    out_ref[:, :width] = lax.dot_general(
        rows, own_ref[...], CONTRACT_LAST, preferred_element_type=jnp.float32
    )
    out_ref[:, width:] = lax.dot_general(
        rows, got_ref[...], CONTRACT_LAST, preferred_element_type=jnp.float32
    )


def place_body(spots_ref, *refs):
    *blocks, out_ref = refs
    for block, block_ref in enumerate(blocks):
        count = block_ref.shape[0]
        out_ref[pl.ds(pl.multiple_of(spots_ref[block] * count, count), count), :] = block_ref[...]


def delta_body(parts_ref, slope_ref, out_ref):
    total = parts_ref[0]
    for part in range(1, parts_ref.shape[0]):
        total = total + parts_ref[part]
    delta = (total * slope_ref[...]).astype(out_ref.dtype)
    for copy in range(out_ref.shape[0]):
        out_ref[copy] = delta


def in_grad_body(delta_ref, own_ref, got_ref, out_ref):
    width = own_ref.shape[1]
    total = lax.dot_general(
        delta_ref[:, :width], own_ref[...], CONTRACT_LAST, preferred_element_type=jnp.float32
    )
    total = total + lax.dot_general(
        delta_ref[:, width:], got_ref[...], CONTRACT_LAST, preferred_element_type=jnp.float32
    )
    out_ref[...] = total.astype(out_ref.dtype)


def sum_body(parts_ref, out_ref):
    total = parts_ref[0].astype(jnp.float32)
    for part in range(1, parts_ref.shape[0]):
        total = total + parts_ref[part].astype(jnp.float32)
    out_ref[...] = total.astype(out_ref.dtype)


def over_tokens(left, right):
    return lax.dot_general(left, right, CONTRACT_FIRST, preferred_element_type=jnp.float32)


def w_in_grad_body(scale, rows_ref, rows_got_ref, delta_ref, delta_got_ref, mask_ref, out_ref):
    grad = over_tokens(rows_ref[...], delta_ref[...])
    grad = grad + over_tokens(rows_got_ref[...], delta_got_ref[...])
    out_ref[...] = (grad * scale * mask_ref[...].astype(jnp.float32)).astype(out_ref.dtype)


def w_out_grad_body(scale, act_ref, act_other_ref, rows_ref, rows_got_ref, mask_ref, out_ref):
    grad = over_tokens(act_ref[...], rows_ref[...])
    grad = grad + over_tokens(act_other_ref[...], rows_got_ref[...])
    out_ref[...] = (grad * scale * mask_ref[...].astype(jnp.float32)).astype(out_ref.dtype)


def shards(n_hid, n_row, inputs, out_grad, pre_act, w_in, w_out, pattern_in, pattern_out):
    far_groups, near_groups = groups(n_hid)
    far = n_hid // 2 // NEAR
    tokens, width = pre_act.shape
    own, features = out_grad.shape
    half = tokens // 2
    share = half // n_row
    runs = share // own
    core = lax.axis_index("hid") % 2
    row = lax.axis_index("row")
    struct = jax.ShapeDtypeStruct

    other = 1 - core

    def partner(x):
        return lax.ppermute(x, "hid", [(i, i ^ 1) for i in range(n_hid)])

    mask_in = widen(pattern_in, BLOCK)
    mask_out = widen(pattern_out, BLOCK)
    w_in_eff = w_in * mask_in
    w_out_eff = w_out * mask_out
    w_in_got = partner(w_in_eff)
    w_out_got = partner(w_out_eff)
    placed = pre_act.reshape(far, NEAR, 2, own, width)
    first = (row % (far // runs)) * runs
    mine = lax.dynamic_slice_in_dim(placed, first, runs, 0)
    mine = lax.dynamic_index_in_dim(mine, row // (far // runs), 1, keepdims=False)
    pre_own = lax.dynamic_index_in_dim(mine, core, 1, keepdims=False).reshape(share, width)
    pre_other = lax.dynamic_index_in_dim(mine, other, 1, keepdims=False).reshape(share, width)
    _, slope = gelu_parts(jnp.concatenate([pre_own, partner(pre_other)], axis=1))

    both = jnp.concatenate([out_grad, inputs], axis=1)
    rows = swap(jnp.broadcast_to(both[None], (far, own, 2 * features)), "hid", far_groups)
    rows, w_out_got, w_in_got, slope, w_in_eff, w_out_eff = lax.optimization_barrier(
        (rows, w_out_got, w_in_got, slope, w_in_eff, w_out_eff)
    )
    rows = rows.reshape(far * own, 2 * features)
    in_block = rows[:, features:]
    rows = jnp.broadcast_to(rows[None, :, :features], (NEAR, far * own, features))
    rows = swap(rows, "hid", near_groups).reshape(half, features)

    n = lax.axis_index("hid") // 2 % NEAR
    steps = [0, 1, NEAR - 1, 2]
    spots = jnp.stack([(n + NEAR - step) % NEAR for step in steps]).astype(jnp.int32)

    def shifted(step):
        step = step - NEAR if step == NEAR - 1 else step
        pairs = [(i, (i + 2 * step) % n_hid) for i in range(n_hid)]
        return lax.ppermute(in_block, "hid", pairs)

    in_blocks = [in_block] + [shifted(step) for step in steps[1:]]

    partial = local(
        act_grad_body,
        struct((half, 2 * width), jnp.float32),
        4 * half * features * width,
        rows,
        w_out_eff,
        w_out_got,
    )
    parts = swap(partial.reshape(n_row, share, 2 * width), "row")
    copies = local(
        delta_body,
        struct((n_row, share, 2 * width), jnp.bfloat16),
        n_row * share * width,
        parts,
        slope,
    )
    delta = swap(copies, "row").reshape(half, 2 * width)

    back = local(
        in_grad_body,
        struct((half, features), jnp.bfloat16),
        4 * half * features * width,
        delta,
        w_in_eff,
        w_in_got,
    )
    back = swap(back.reshape(NEAR, far * own, features), "hid", near_groups)
    back, in_blocks[1] = lax.optimization_barrier((back, in_blocks[1]))
    back = local(sum_body, struct((far * own, features), jnp.bfloat16), back.size, back)
    back = swap(back.reshape(far, own, features), "hid", far_groups)
    in_grad = local(sum_body, struct((own, features), jnp.bfloat16), back.size, back)

    in_rows = pl.pallas_call(
        place_body,
        out_shape=struct((half, features), jnp.bfloat16),
        in_specs=[pl.BlockSpec(memory_space=pltpu.SMEM)]
        + [pl.BlockSpec(memory_space=pltpu.VMEM)] * NEAR,
        out_specs=pl.BlockSpec(memory_space=pltpu.VMEM),
        compiler_params=pltpu.CompilerParams(vmem_limit_bytes=24 * 2**20),
        cost_estimate=pl.CostEstimate(
            flops=0, bytes_accessed=4 * half * features, transcendentals=0
        ),
    )(spots, *in_blocks)

    scale = 1.0 / math.sqrt(tokens)
    w_in_grad = local(
        lambda *refs: w_in_grad_body(scale, *refs),
        struct((features, width), jnp.bfloat16),
        2 * tokens * features * width,
        in_rows,
        partner(in_rows),
        delta[:, :width],
        partner(delta[:, width:]),
        mask_in,
    )
    value, _ = gelu_parts(placed.transpose(2, 1, 0, 3, 4).reshape(2, half, width))
    act = value.astype(jnp.bfloat16)
    w_out_grad = local(
        lambda *refs: w_out_grad_body(scale, *refs),
        struct((width, features), jnp.bfloat16),
        2 * tokens * features * width,
        lax.dynamic_index_in_dim(act, core, 0, keepdims=False),
        lax.dynamic_index_in_dim(act, other, 0, keepdims=False),
        rows,
        partner(rows),
        mask_out,
    )
    return (in_grad, w_in_grad, w_out_grad)


def solution(mesh):
    placed = (
        P("hid", "row"),
        P("hid", "row"),
        P(None, "hid"),
        P("row", "hid"),
        P("hid", "row"),
        P("row", "hid"),
        P("hid", "row"),
    )
    return jax.shard_map(
        lambda *blocks: shards(mesh.shape["hid"], mesh.shape["row"], *blocks),
        mesh=mesh,
        in_specs=placed,
        out_specs=(P("hid", "row"), P("row", "hid"), P("hid", "row")),
        check_vma=False,
    )
```

```python
import math

import jax
import jax.numpy as jnp
from jax import lax
from jax.experimental import pallas as pl
from jax.experimental.pallas import tpu as pltpu
from jax.sharding import PartitionSpec as P

BLOCK = 128
NEAR = 4
CONTRACT_LAST = (((1,), (1,)), ((), ()))
CONTRACT_FIRST = (((0,), (0,)), ((), ()))


def widen(pattern, block):
    rows, cols = pattern.shape
    wide = jnp.broadcast_to(
        pattern.astype(jnp.bfloat16)[:, None, :, None], (rows, block, cols, block)
    )
    return wide.reshape(rows * block, cols * block)


def gelu_parts(pre_act):
    values = pre_act.astype(jnp.float32)
    return jax.jvp(lambda v: jax.nn.gelu(v, approximate=True), (values,), (jnp.ones_like(values),))


def groups(n_hid):
    far = n_hid // 2 // NEAR
    at = lambda k, n, c: 2 * (NEAR * k + n) + c
    return (
        [[at(k, n, c) for k in range(far)] for n in range(NEAR) for c in range(2)],
        [[at(k, n, c) for n in range(NEAR)] for k in range(far) for c in range(2)],
    )


def swap(x, axis, within=None):
    return lax.all_to_all(x, axis, 0, 0, axis_index_groups=within, tiled=True)


def local(body, out_shape, flops, *args):
    size = sum(a.size * a.dtype.itemsize for a in (*args, out_shape))
    return pl.pallas_call(
        body,
        out_shape=out_shape,
        in_specs=[pl.BlockSpec(memory_space=pltpu.VMEM)] * len(args),
        out_specs=pl.BlockSpec(memory_space=pltpu.VMEM),
        compiler_params=pltpu.CompilerParams(vmem_limit_bytes=24 * 2**20),
        cost_estimate=pl.CostEstimate(flops=flops, bytes_accessed=size, transcendentals=0),
    )(*args)


def act_grad_body(rows_ref, own_ref, got_ref, out_ref):
    width = own_ref.shape[0]
    rows = rows_ref[...]
    for place, weight_ref in ((0, own_ref), (width, got_ref)):
        partial = lax.dot_general(
            rows, weight_ref[...], CONTRACT_LAST, preferred_element_type=jnp.float32
        )
        out_ref[:, place : place + width] = partial.astype(out_ref.dtype)


def place_body(spots_ref, *refs):
    *blocks, out_ref = refs
    for block, block_ref in enumerate(blocks):
        count = block_ref.shape[0]
        out_ref[pl.ds(pl.multiple_of(spots_ref[block] * count, count), count), :] = block_ref[...]


def delta_body(parts_ref, slope_ref, out_ref):
    total = parts_ref[0].astype(jnp.float32)
    for part in range(1, parts_ref.shape[0]):
        total = total + parts_ref[part].astype(jnp.float32)
    delta = (total * slope_ref[...]).astype(out_ref.dtype)
    for copy in range(out_ref.shape[0]):
        out_ref[copy] = delta


def in_grad_body(delta_ref, own_ref, got_ref, out_ref):
    width = own_ref.shape[1]
    total = lax.dot_general(
        delta_ref[:, :width], own_ref[...], CONTRACT_LAST, preferred_element_type=jnp.float32
    )
    total = total + lax.dot_general(
        delta_ref[:, width:], got_ref[...], CONTRACT_LAST, preferred_element_type=jnp.float32
    )
    out_ref[...] = total.astype(out_ref.dtype)


def sum_body(parts_ref, out_ref):
    total = parts_ref[0].astype(jnp.float32)
    for part in range(1, parts_ref.shape[0]):
        total = total + parts_ref[part].astype(jnp.float32)
    out_ref[...] = total.astype(out_ref.dtype)


def over_tokens(left, right):
    return lax.dot_general(left, right, CONTRACT_FIRST, preferred_element_type=jnp.float32)


def w_in_grad_body(scale, rows_ref, rows_got_ref, delta_ref, delta_got_ref, mask_ref, out_ref):
    grad = over_tokens(rows_ref[...], delta_ref[...])
    grad = grad + over_tokens(rows_got_ref[...], delta_got_ref[...])
    out_ref[...] = (grad * scale * mask_ref[...].astype(jnp.float32)).astype(out_ref.dtype)


def w_out_grad_body(scale, act_ref, act_other_ref, rows_ref, rows_got_ref, mask_ref, out_ref):
    grad = over_tokens(act_ref[...], rows_ref[...])
    grad = grad + over_tokens(act_other_ref[...], rows_got_ref[...])
    out_ref[...] = (grad * scale * mask_ref[...].astype(jnp.float32)).astype(out_ref.dtype)


def shards(n_hid, n_row, inputs, out_grad, pre_act, w_in, w_out, pattern_in, pattern_out):
    far_groups, near_groups = groups(n_hid)
    far = n_hid // 2 // NEAR
    tokens, width = pre_act.shape
    own, features = out_grad.shape
    half = tokens // 2
    share = half // n_row
    runs = share // own
    core = lax.axis_index("hid") % 2
    row = lax.axis_index("row")
    struct = jax.ShapeDtypeStruct

    other = 1 - core

    def partner(x):
        return lax.ppermute(x, "hid", [(i, i ^ 1) for i in range(n_hid)])

    mask_in = widen(pattern_in, BLOCK)
    mask_out = widen(pattern_out, BLOCK)
    w_in_eff = w_in * mask_in
    w_out_eff = w_out * mask_out
    w_in_got = partner(w_in_eff)
    w_out_got = partner(w_out_eff)
    placed = pre_act.reshape(far, NEAR, 2, own, width)
    first = (row % (far // runs)) * runs
    mine = lax.dynamic_slice_in_dim(placed, first, runs, 0)
    mine = lax.dynamic_index_in_dim(mine, row // (far // runs), 1, keepdims=False)
    pre_own = lax.dynamic_index_in_dim(mine, core, 1, keepdims=False).reshape(share, width)
    pre_other = lax.dynamic_index_in_dim(mine, other, 1, keepdims=False).reshape(share, width)
    _, slope = gelu_parts(jnp.concatenate([pre_own, partner(pre_other)], axis=1))

    value, _ = gelu_parts(pre_act)
    act = value.astype(jnp.bfloat16).reshape(placed.shape)
    act = act.transpose(2, 1, 0, 3, 4).reshape(2, half, width)

    both = jnp.concatenate([out_grad, inputs], axis=1)
    rows = swap(jnp.broadcast_to(both[None], (far, own, 2 * features)), "hid", far_groups)
    rows, w_out_got, w_in_got, slope, w_in_eff, w_out_eff, act = lax.optimization_barrier(
        (rows, w_out_got, w_in_got, slope, w_in_eff, w_out_eff, act)
    )
    rows = rows.reshape(far * own, 2 * features)
    in_block = rows[:, features:]
    rows = jnp.broadcast_to(rows[None, :, :features], (NEAR, far * own, features))
    rows = swap(rows, "hid", near_groups).reshape(half, features)

    n = lax.axis_index("hid") // 2 % NEAR
    steps = [0, 1, NEAR - 1, 2]
    spots = jnp.stack([(n + NEAR - step) % NEAR for step in steps]).astype(jnp.int32)

    def shifted(step):
        step = step - NEAR if step == NEAR - 1 else step
        pairs = [(i, (i + 2 * step) % n_hid) for i in range(n_hid)]
        return lax.ppermute(in_block, "hid", pairs)

    in_blocks = [in_block] + [shifted(step) for step in steps[1:]]

    partial = local(
        act_grad_body,
        struct((half, 2 * width), jnp.bfloat16),
        4 * half * features * width,
        rows,
        w_out_eff,
        w_out_got,
    )
    parts = swap(partial.reshape(n_row, share, 2 * width), "row")
    copies = local(
        delta_body,
        struct((n_row, share, 2 * width), jnp.bfloat16),
        n_row * share * width,
        parts,
        slope,
    )
    delta = swap(copies, "row").reshape(half, 2 * width)

    back = local(
        in_grad_body,
        struct((half, features), jnp.bfloat16),
        4 * half * features * width,
        delta,
        w_in_eff,
        w_in_got,
    )
    back = swap(back.reshape(NEAR, far * own, features), "hid", near_groups)
    back, in_blocks[1] = lax.optimization_barrier((back, in_blocks[1]))
    back = local(sum_body, struct((far * own, features), jnp.bfloat16), back.size, back)
    back = swap(back.reshape(far, own, features), "hid", far_groups)
    in_grad = local(sum_body, struct((own, features), jnp.bfloat16), back.size, back)

    in_rows = pl.pallas_call(
        place_body,
        out_shape=struct((half, features), jnp.bfloat16),
        in_specs=[pl.BlockSpec(memory_space=pltpu.SMEM)]
        + [pl.BlockSpec(memory_space=pltpu.VMEM)] * NEAR,
        out_specs=pl.BlockSpec(memory_space=pltpu.VMEM),
        compiler_params=pltpu.CompilerParams(vmem_limit_bytes=24 * 2**20),
        cost_estimate=pl.CostEstimate(
            flops=0, bytes_accessed=4 * half * features, transcendentals=0
        ),
    )(spots, *in_blocks)

    scale = 1.0 / math.sqrt(tokens)
    w_in_grad = local(
        lambda *refs: w_in_grad_body(scale, *refs),
        struct((features, width), jnp.bfloat16),
        2 * tokens * features * width,
        in_rows,
        partner(in_rows),
        delta[:, :width],
        partner(delta[:, width:]),
        mask_in,
    )
    w_out_grad = local(
        lambda *refs: w_out_grad_body(scale, *refs),
        struct((width, features), jnp.bfloat16),
        2 * tokens * features * width,
        lax.dynamic_index_in_dim(act, core, 0, keepdims=False),
        lax.dynamic_index_in_dim(act, other, 0, keepdims=False),
        rows,
        partner(rows),
        mask_out,
    )
    return (in_grad, w_in_grad, w_out_grad)


def solution(mesh):
    placed = (
        P("hid", "row"),
        P("hid", "row"),
        P(None, "hid"),
        P("row", "hid"),
        P("hid", "row"),
        P("row", "hid"),
        P("hid", "row"),
    )
    return jax.shard_map(
        lambda *blocks: shards(mesh.shape["hid"], mesh.shape["row"], *blocks),
        mesh=mesh,
        in_specs=placed,
        out_specs=(P("hid", "row"), P("row", "hid"), P("hid", "row")),
        check_vma=False,
    )
```

```python
import math

import jax
import jax.numpy as jnp
from jax import lax
from jax.experimental import pallas as pl
from jax.experimental.pallas import tpu as pltpu
from jax.sharding import PartitionSpec as P

BLOCK = 128
NEAR = 4
CONTRACT_LAST = (((1,), (1,)), ((), ()))
CONTRACT_FIRST = (((0,), (0,)), ((), ()))


def widen(pattern, block):
    rows, cols = pattern.shape
    wide = jnp.broadcast_to(
        pattern.astype(jnp.bfloat16)[:, None, :, None], (rows, block, cols, block)
    )
    return wide.reshape(rows * block, cols * block)


def gelu_parts(pre_act):
    values = pre_act.astype(jnp.float32)
    return jax.jvp(lambda v: jax.nn.gelu(v, approximate=True), (values,), (jnp.ones_like(values),))


def groups(n_hid):
    far = n_hid // 2 // NEAR
    at = lambda k, n, c: 2 * (NEAR * k + n) + c
    return (
        [[at(k, n, c) for k in range(far)] for n in range(NEAR) for c in range(2)],
        [[at(k, n, c) for n in range(NEAR)] for k in range(far) for c in range(2)],
    )


def swap(x, axis, within=None):
    return lax.all_to_all(x, axis, 0, 0, axis_index_groups=within, tiled=True)


def local(body, out_shape, flops, *args):
    size = sum(a.size * a.dtype.itemsize for a in (*args, out_shape))
    return pl.pallas_call(
        body,
        out_shape=out_shape,
        in_specs=[pl.BlockSpec(memory_space=pltpu.VMEM)] * len(args),
        out_specs=pl.BlockSpec(memory_space=pltpu.VMEM),
        compiler_params=pltpu.CompilerParams(vmem_limit_bytes=24 * 2**20),
        cost_estimate=pl.CostEstimate(flops=flops, bytes_accessed=size, transcendentals=0),
    )(*args)


def act_grad_body(rows_ref, own_ref, got_ref, out_ref):
    width = own_ref.shape[0]
    rows = rows_ref[...]
    for place, weight_ref in ((0, own_ref), (width, got_ref)):
        partial = lax.dot_general(
            rows, weight_ref[...], CONTRACT_LAST, preferred_element_type=jnp.float32
        )
        out_ref[:, place : place + width] = partial.astype(out_ref.dtype)


def place_body(spots_ref, *refs):
    *blocks, out_ref = refs
    for block, block_ref in enumerate(blocks):
        count = block_ref.shape[0]
        out_ref[pl.ds(pl.multiple_of(spots_ref[block] * count, count), count), :] = block_ref[...]


def delta_body(parts_ref, slope_ref, out_ref):
    total = parts_ref[0].astype(jnp.float32)
    for part in range(1, parts_ref.shape[0]):
        total = total + parts_ref[part].astype(jnp.float32)
    delta = (total * slope_ref[...]).astype(out_ref.dtype)
    for copy in range(out_ref.shape[0]):
        out_ref[copy] = delta


def in_grad_body(delta_ref, own_ref, got_ref, out_ref):
    width = own_ref.shape[1]
    total = lax.dot_general(
        delta_ref[:, :width], own_ref[...], CONTRACT_LAST, preferred_element_type=jnp.float32
    )
    total = total + lax.dot_general(
        delta_ref[:, width:], got_ref[...], CONTRACT_LAST, preferred_element_type=jnp.float32
    )
    out_ref[...] = total.astype(out_ref.dtype)


def sum_body(parts_ref, out_ref):
    total = parts_ref[0].astype(jnp.float32)
    for part in range(1, parts_ref.shape[0]):
        total = total + parts_ref[part].astype(jnp.float32)
    out_ref[...] = total.astype(out_ref.dtype)


def over_tokens(left, right):
    return lax.dot_general(left, right, CONTRACT_FIRST, preferred_element_type=jnp.float32)


def w_in_grad_body(scale, rows_ref, rows_got_ref, delta_ref, delta_got_ref, mask_ref, out_ref):
    grad = over_tokens(rows_ref[...], delta_ref[...])
    grad = grad + over_tokens(rows_got_ref[...], delta_got_ref[...])
    out_ref[...] = (grad * scale * mask_ref[...].astype(jnp.float32)).astype(out_ref.dtype)


def w_out_grad_body(scale, act_ref, act_other_ref, rows_ref, rows_got_ref, mask_ref, out_ref):
    grad = over_tokens(act_ref[...], rows_ref[...])
    grad = grad + over_tokens(act_other_ref[...], rows_got_ref[...])
    out_ref[...] = (grad * scale * mask_ref[...].astype(jnp.float32)).astype(out_ref.dtype)


def shards(n_hid, n_row, inputs, out_grad, pre_act, w_in, w_out, pattern_in, pattern_out):
    far_groups, near_groups = groups(n_hid)
    far = n_hid // 2 // NEAR
    tokens, width = pre_act.shape
    own, features = out_grad.shape
    half = tokens // 2
    share = half // n_row
    runs = share // own
    core = lax.axis_index("hid") % 2
    row = lax.axis_index("row")
    struct = jax.ShapeDtypeStruct

    other = 1 - core

    def partner(x):
        return lax.ppermute(x, "hid", [(i, i ^ 1) for i in range(n_hid)])

    mask_in = widen(pattern_in, BLOCK)
    mask_out = widen(pattern_out, BLOCK)
    w_in_eff = w_in * mask_in
    w_out_eff = w_out * mask_out
    w_in_got = partner(w_in_eff)
    w_out_got = partner(w_out_eff)
    placed = pre_act.reshape(far, NEAR, 2, own, width)
    first = (row % (far // runs)) * runs
    mine = lax.dynamic_slice_in_dim(placed, first, runs, 0)
    mine = lax.dynamic_index_in_dim(mine, row // (far // runs), 1, keepdims=False)
    pre_own = lax.dynamic_index_in_dim(mine, core, 1, keepdims=False).reshape(share, width)
    pre_other = lax.dynamic_index_in_dim(mine, other, 1, keepdims=False).reshape(share, width)
    _, slope = gelu_parts(jnp.concatenate([pre_own, partner(pre_other)], axis=1))

    value, _ = gelu_parts(pre_act)
    act = value.astype(jnp.bfloat16).reshape(placed.shape)
    act = act.transpose(2, 1, 0, 3, 4).reshape(2, half, width)

    both = jnp.concatenate([out_grad, inputs], axis=1)
    rows = swap(jnp.broadcast_to(both[None], (far, own, 2 * features)), "hid", far_groups)
    rows, w_out_got, w_in_got, slope, w_in_eff, w_out_eff, act = lax.optimization_barrier(
        (rows, w_out_got, w_in_got, slope, w_in_eff, w_out_eff, act)
    )
    rows = rows.reshape(far * own, 2 * features)
    in_block = rows[:, features:]
    rows = jnp.broadcast_to(rows[None, :, :features], (NEAR, far * own, features))
    rows = swap(rows, "hid", near_groups).reshape(half, features)

    n = lax.axis_index("hid") // 2 % NEAR
    steps = [0, 1, NEAR - 1, 2]
    spots = jnp.stack([(n + NEAR - step) % NEAR for step in steps]).astype(jnp.int32)

    def shifted(step):
        step = step - NEAR if step == NEAR - 1 else step
        pairs = [(i, (i + 2 * step) % n_hid) for i in range(n_hid)]
        return lax.ppermute(in_block, "hid", pairs)

    in_blocks = [in_block] + [shifted(step) for step in steps[1:]]

    partial = local(
        act_grad_body,
        struct((half, 2 * width), jnp.bfloat16),
        4 * half * features * width,
        rows,
        w_out_eff,
        w_out_got,
    )
    parts = swap(partial.reshape(n_row, share, 2 * width), "row")
    parts, *in_blocks[1:3] = lax.optimization_barrier((parts, *in_blocks[1:3]))
    copies = local(
        delta_body,
        struct((n_row, share, 2 * width), jnp.bfloat16),
        n_row * share * width,
        parts,
        slope,
    )
    delta = swap(copies, "row").reshape(half, 2 * width)

    back = local(
        in_grad_body,
        struct((half, features), jnp.bfloat16),
        4 * half * features * width,
        delta,
        w_in_eff,
        w_in_got,
    )
    back = swap(back.reshape(NEAR, far * own, features), "hid", near_groups)
    scale = 1.0 / math.sqrt(tokens)
    delta_got = partner(delta[:, width:])
    w_out_grad = local(
        lambda *refs: w_out_grad_body(scale, *refs),
        struct((width, features), jnp.bfloat16),
        2 * tokens * features * width,
        lax.dynamic_index_in_dim(act, core, 0, keepdims=False),
        lax.dynamic_index_in_dim(act, other, 0, keepdims=False),
        rows,
        partner(rows),
        mask_out,
    )
    back, delta_got, w_out_grad = lax.optimization_barrier((back, delta_got, w_out_grad))
    back = local(sum_body, struct((far * own, features), jnp.bfloat16), back.size, back)
    back = swap(back.reshape(far, own, features), "hid", far_groups)
    in_grad = local(sum_body, struct((own, features), jnp.bfloat16), back.size, back)

    in_rows = pl.pallas_call(
        place_body,
        out_shape=struct((half, features), jnp.bfloat16),
        in_specs=[pl.BlockSpec(memory_space=pltpu.SMEM)]
        + [pl.BlockSpec(memory_space=pltpu.VMEM)] * NEAR,
        out_specs=pl.BlockSpec(memory_space=pltpu.VMEM),
        compiler_params=pltpu.CompilerParams(vmem_limit_bytes=24 * 2**20),
        cost_estimate=pl.CostEstimate(
            flops=0, bytes_accessed=4 * half * features, transcendentals=0
        ),
    )(spots, *in_blocks)

    w_in_grad = local(
        lambda *refs: w_in_grad_body(scale, *refs),
        struct((features, width), jnp.bfloat16),
        2 * tokens * features * width,
        in_rows,
        partner(in_rows),
        delta[:, :width],
        delta_got,
        mask_in,
    )
    return (in_grad, w_in_grad, w_out_grad)


def solution(mesh):
    placed = (
        P("hid", "row"),
        P("hid", "row"),
        P(None, "hid"),
        P("row", "hid"),
        P("hid", "row"),
        P("row", "hid"),
        P("hid", "row"),
    )
    return jax.shard_map(
        lambda *blocks: shards(mesh.shape["hid"], mesh.shape["row"], *blocks),
        mesh=mesh,
        in_specs=placed,
        out_specs=(P("hid", "row"), P("row", "hid"), P("hid", "row")),
        check_vma=False,
    )
```

```python
import math

import jax
import jax.numpy as jnp
from jax import lax
from jax.experimental import pallas as pl
from jax.experimental.pallas import tpu as pltpu
from jax.sharding import PartitionSpec as P

BLOCK = 128
NEAR = 4
CONTRACT_LAST = (((1,), (1,)), ((), ()))
CONTRACT_FIRST = (((0,), (0,)), ((), ()))


def widen(pattern, block):
    rows, cols = pattern.shape
    wide = jnp.broadcast_to(
        pattern.astype(jnp.bfloat16)[:, None, :, None], (rows, block, cols, block)
    )
    return wide.reshape(rows * block, cols * block)


def gelu_parts(pre_act):
    values = pre_act.astype(jnp.float32)
    return jax.jvp(lambda v: jax.nn.gelu(v, approximate=True), (values,), (jnp.ones_like(values),))


def groups(n_hid):
    far = n_hid // 2 // NEAR
    at = lambda k, n, c: 2 * (NEAR * k + n) + c
    return (
        [[at(k, n, c) for k in range(far)] for n in range(NEAR) for c in range(2)],
        [[at(k, n, c) for n in range(NEAR)] for k in range(far) for c in range(2)],
    )


def swap(x, axis, within=None):
    return lax.all_to_all(x, axis, 0, 0, axis_index_groups=within, tiled=True)


def local(body, out_shape, flops, *args):
    size = sum(a.size * a.dtype.itemsize for a in (*args, out_shape))
    return pl.pallas_call(
        body,
        out_shape=out_shape,
        in_specs=[pl.BlockSpec(memory_space=pltpu.VMEM)] * len(args),
        out_specs=pl.BlockSpec(memory_space=pltpu.VMEM),
        compiler_params=pltpu.CompilerParams(vmem_limit_bytes=24 * 2**20),
        cost_estimate=pl.CostEstimate(flops=flops, bytes_accessed=size, transcendentals=0),
    )(*args)


def act_grad_body(rows_ref, own_ref, got_ref, out_ref):
    width = own_ref.shape[0]
    rows = rows_ref[...]
    for place, weight_ref in ((0, own_ref), (width, got_ref)):
        partial = lax.dot_general(
            rows, weight_ref[...], CONTRACT_LAST, preferred_element_type=jnp.float32
        )
        out_ref[:, place : place + width] = partial.astype(out_ref.dtype)


def place_body(spots_ref, *refs):
    *blocks, out_ref = refs
    for block, block_ref in enumerate(blocks):
        count = block_ref.shape[0]
        out_ref[pl.ds(pl.multiple_of(spots_ref[block] * count, count), count), :] = block_ref[...]


def delta_body(parts_ref, slope_ref, out_ref):
    total = parts_ref[0].astype(jnp.float32)
    for part in range(1, parts_ref.shape[0]):
        total = total + parts_ref[part].astype(jnp.float32)
    delta = (total * slope_ref[...]).astype(out_ref.dtype)
    for copy in range(out_ref.shape[0]):
        out_ref[copy] = delta


def in_grad_body(delta_ref, own_ref, got_ref, out_ref):
    width = own_ref.shape[1]
    total = lax.dot_general(
        delta_ref[:, :width], own_ref[...], CONTRACT_LAST, preferred_element_type=jnp.float32
    )
    total = total + lax.dot_general(
        delta_ref[:, width:], got_ref[...], CONTRACT_LAST, preferred_element_type=jnp.float32
    )
    out_ref[...] = total.astype(out_ref.dtype)


def sum_body(parts_ref, out_ref):
    total = parts_ref[0].astype(jnp.float32)
    for part in range(1, parts_ref.shape[0]):
        total = total + parts_ref[part].astype(jnp.float32)
    out_ref[...] = total.astype(out_ref.dtype)


def over_tokens(left, right):
    return lax.dot_general(left, right, CONTRACT_FIRST, preferred_element_type=jnp.float32)


def w_in_grad_body(scale, rows_ref, rows_got_ref, delta_ref, delta_got_ref, mask_ref, out_ref):
    grad = over_tokens(rows_ref[...], delta_ref[...])
    grad = grad + over_tokens(rows_got_ref[...], delta_got_ref[...])
    out_ref[...] = (grad * scale * mask_ref[...].astype(jnp.float32)).astype(out_ref.dtype)


def w_out_grad_body(scale, act_ref, act_other_ref, rows_ref, rows_got_ref, mask_ref, out_ref):
    grad = over_tokens(act_ref[...], rows_ref[...])
    grad = grad + over_tokens(act_other_ref[...], rows_got_ref[...])
    out_ref[...] = (grad * scale * mask_ref[...].astype(jnp.float32)).astype(out_ref.dtype)


def shards(n_hid, n_row, inputs, out_grad, pre_act, w_in, w_out, pattern_in, pattern_out):
    far_groups, near_groups = groups(n_hid)
    far = n_hid // 2 // NEAR
    tokens, width = pre_act.shape
    own, features = out_grad.shape
    half = tokens // 2
    share = half // n_row
    runs = share // own
    core = lax.axis_index("hid") % 2
    row = lax.axis_index("row")
    struct = jax.ShapeDtypeStruct

    other = 1 - core

    def partner(x):
        return lax.ppermute(x, "hid", [(i, i ^ 1) for i in range(n_hid)])

    mask_in = widen(pattern_in, BLOCK)
    mask_out = widen(pattern_out, BLOCK)
    w_in_eff = w_in * mask_in
    w_out_eff = w_out * mask_out
    w_in_got = partner(w_in_eff)
    w_out_got = partner(w_out_eff)
    placed = pre_act.reshape(far, NEAR, 2, own, width)
    first = (row % (far // runs)) * runs
    mine = lax.dynamic_slice_in_dim(placed, first, runs, 0)
    mine = lax.dynamic_index_in_dim(mine, row // (far // runs), 1, keepdims=False)
    pre_own = lax.dynamic_index_in_dim(mine, core, 1, keepdims=False).reshape(share, width)
    pre_other = lax.dynamic_index_in_dim(mine, other, 1, keepdims=False).reshape(share, width)
    _, slope = gelu_parts(jnp.concatenate([pre_own, partner(pre_other)], axis=1))

    value, _ = gelu_parts(pre_act)
    act = value.astype(jnp.bfloat16).reshape(placed.shape)
    act = act.transpose(2, 1, 0, 3, 4).reshape(2, half, width)

    both = jnp.concatenate([out_grad, inputs], axis=1)
    rows = swap(jnp.broadcast_to(both[None], (far, own, 2 * features)), "hid", far_groups)
    rows, w_out_got, w_in_got, slope, w_in_eff, w_out_eff, act = lax.optimization_barrier(
        (rows, w_out_got, w_in_got, slope, w_in_eff, w_out_eff, act)
    )
    rows = rows.reshape(far * own, 2 * features)
    in_block = rows[:, features:]
    rows = jnp.broadcast_to(rows[None, :, :features], (NEAR, far * own, features))
    rows = swap(rows, "hid", near_groups).reshape(half, features)

    n = lax.axis_index("hid") // 2 % NEAR
    steps = [0, 1, NEAR - 1, 2]
    spots = jnp.stack([(n + NEAR - step) % NEAR for step in steps]).astype(jnp.int32)

    def shifted(step):
        step = step - NEAR if step == NEAR - 1 else step
        pairs = [(i, (i + 2 * step) % n_hid) for i in range(n_hid)]
        return lax.ppermute(in_block, "hid", pairs)

    in_blocks = [in_block] + [shifted(step) for step in steps[1:]]

    partial = local(
        act_grad_body,
        struct((half, 2 * width), jnp.bfloat16),
        4 * half * features * width,
        rows,
        w_out_eff,
        w_out_got,
    )
    parts = swap(partial.reshape(n_row, share, 2 * width), "row")
    copies = local(
        delta_body,
        struct((n_row, share, 2 * width), jnp.bfloat16),
        n_row * share * width,
        parts,
        slope,
    )
    delta = swap(copies, "row").reshape(half, 2 * width)

    back = local(
        in_grad_body,
        struct((half, features), jnp.bfloat16),
        4 * half * features * width,
        delta,
        w_in_eff,
        w_in_got,
    )
    back = swap(back.reshape(NEAR, far * own, features), "hid", near_groups)
    scale = 1.0 / math.sqrt(tokens)
    delta_got = partner(delta[:, width:])
    w_out_grad = local(
        lambda *refs: w_out_grad_body(scale, *refs),
        struct((width, features), jnp.bfloat16),
        2 * tokens * features * width,
        lax.dynamic_index_in_dim(act, core, 0, keepdims=False),
        lax.dynamic_index_in_dim(act, other, 0, keepdims=False),
        rows,
        partner(rows),
        mask_out,
    )
    back, delta_got, w_out_grad = lax.optimization_barrier((back, delta_got, w_out_grad))
    back = local(sum_body, struct((far * own, features), jnp.bfloat16), back.size, back)
    back = swap(back.reshape(far, own, features), "hid", far_groups)
    in_grad = local(sum_body, struct((own, features), jnp.bfloat16), back.size, back)

    in_rows = pl.pallas_call(
        place_body,
        out_shape=struct((half, features), jnp.bfloat16),
        in_specs=[pl.BlockSpec(memory_space=pltpu.SMEM)]
        + [pl.BlockSpec(memory_space=pltpu.VMEM)] * NEAR,
        out_specs=pl.BlockSpec(memory_space=pltpu.VMEM),
        compiler_params=pltpu.CompilerParams(vmem_limit_bytes=24 * 2**20),
        cost_estimate=pl.CostEstimate(
            flops=0, bytes_accessed=4 * half * features, transcendentals=0
        ),
    )(spots, *in_blocks)

    w_in_grad = local(
        lambda *refs: w_in_grad_body(scale, *refs),
        struct((features, width), jnp.bfloat16),
        2 * tokens * features * width,
        in_rows,
        partner(in_rows),
        delta[:, :width],
        delta_got,
        mask_in,
    )
    return (in_grad, w_in_grad, w_out_grad)


def solution(mesh):
    placed = (
        P("hid", "row"),
        P("hid", "row"),
        P(None, "hid"),
        P("row", "hid"),
        P("hid", "row"),
        P("row", "hid"),
        P("hid", "row"),
    )
    return jax.shard_map(
        lambda *blocks: shards(mesh.shape["hid"], mesh.shape["row"], *blocks),
        mesh=mesh,
        in_specs=placed,
        out_specs=(P("hid", "row"), P("row", "hid"), P("hid", "row")),
        check_vma=False,
    )
```

```python
import math

import jax
import jax.numpy as jnp
from jax import lax
from jax.experimental import pallas as pl
from jax.experimental.pallas import tpu as pltpu
from jax.sharding import PartitionSpec as P

BLOCK = 128
NEAR = 4
CONTRACT_LAST = (((1,), (1,)), ((), ()))
CONTRACT_FIRST = (((0,), (0,)), ((), ()))


def widen(pattern, block):
    rows, cols = pattern.shape
    wide = jnp.broadcast_to(
        pattern.astype(jnp.bfloat16)[:, None, :, None], (rows, block, cols, block)
    )
    return wide.reshape(rows * block, cols * block)


def gelu_parts(pre_act):
    values = pre_act.astype(jnp.float32)
    return jax.jvp(lambda v: jax.nn.gelu(v, approximate=True), (values,), (jnp.ones_like(values),))


def groups(n_hid):
    far = n_hid // 2 // NEAR
    at = lambda k, n, c: 2 * (NEAR * k + n) + c
    return (
        [[at(k, n, c) for k in range(far)] for n in range(NEAR) for c in range(2)],
        [[at(k, n, c) for n in range(NEAR)] for k in range(far) for c in range(2)],
    )


def swap(x, axis, within=None):
    return lax.all_to_all(x, axis, 0, 0, axis_index_groups=within, tiled=True)


def local(body, out_shape, flops, *args):
    size = sum(a.size * a.dtype.itemsize for a in (*args, out_shape))
    return pl.pallas_call(
        body,
        out_shape=out_shape,
        in_specs=[pl.BlockSpec(memory_space=pltpu.VMEM)] * len(args),
        out_specs=pl.BlockSpec(memory_space=pltpu.VMEM),
        compiler_params=pltpu.CompilerParams(vmem_limit_bytes=24 * 2**20),
        cost_estimate=pl.CostEstimate(flops=flops, bytes_accessed=size, transcendentals=0),
    )(*args)


def act_grad_body(rows_ref, own_ref, got_ref, out_ref):
    width = own_ref.shape[0]
    rows = rows_ref[...]
    for place, weight_ref in ((0, own_ref), (width, got_ref)):
        partial = lax.dot_general(
            rows, weight_ref[...], CONTRACT_LAST, preferred_element_type=jnp.float32
        )
        out_ref[:, place : place + width] = partial.astype(out_ref.dtype)


def place_body(spots_ref, *refs):
    *blocks, out_ref = refs
    for block, block_ref in enumerate(blocks):
        count = block_ref.shape[0]
        out_ref[pl.ds(pl.multiple_of(spots_ref[block] * count, count), count), :] = block_ref[...]


def delta_body(parts_ref, slope_ref, out_ref):
    total = parts_ref[0].astype(jnp.float32)
    for part in range(1, parts_ref.shape[0]):
        total = total + parts_ref[part].astype(jnp.float32)
    delta = (total * slope_ref[...]).astype(out_ref.dtype)
    for copy in range(out_ref.shape[0]):
        out_ref[copy] = delta


def in_grad_body(delta_ref, own_ref, got_ref, out_ref):
    width = own_ref.shape[1]
    total = lax.dot_general(
        delta_ref[:, :width], own_ref[...], CONTRACT_LAST, preferred_element_type=jnp.float32
    )
    total = total + lax.dot_general(
        delta_ref[:, width:], got_ref[...], CONTRACT_LAST, preferred_element_type=jnp.float32
    )
    out_ref[...] = total.astype(out_ref.dtype)


def sum_body(parts_ref, out_ref):
    total = parts_ref[0].astype(jnp.float32)
    for part in range(1, parts_ref.shape[0]):
        total = total + parts_ref[part].astype(jnp.float32)
    out_ref[...] = total.astype(out_ref.dtype)


def over_tokens(left, right):
    return lax.dot_general(left, right, CONTRACT_FIRST, preferred_element_type=jnp.float32)


def w_in_grad_body(scale, rows_ref, rows_got_ref, delta_ref, delta_got_ref, mask_ref, out_ref):
    grad = over_tokens(rows_ref[...], delta_ref[...])
    grad = grad + over_tokens(rows_got_ref[...], delta_got_ref[...])
    out_ref[...] = (grad * scale * mask_ref[...].astype(jnp.float32)).astype(out_ref.dtype)


def w_out_grad_body(scale, act_ref, act_other_ref, rows_ref, rows_got_ref, mask_ref, out_ref):
    grad = over_tokens(act_ref[...], rows_ref[...])
    grad = grad + over_tokens(act_other_ref[...], rows_got_ref[...])
    out_ref[...] = (grad * scale * mask_ref[...].astype(jnp.float32)).astype(out_ref.dtype)


def shards(n_hid, n_row, inputs, out_grad, pre_act, w_in, w_out, pattern_in, pattern_out):
    far_groups, near_groups = groups(n_hid)
    far = n_hid // 2 // NEAR
    tokens, width = pre_act.shape
    own, features = out_grad.shape
    half = tokens // 2
    share = half // n_row
    runs = share // own
    core = lax.axis_index("hid") % 2
    row = lax.axis_index("row")
    struct = jax.ShapeDtypeStruct

    other = 1 - core

    def partner(x):
        return lax.ppermute(x, "hid", [(i, i ^ 1) for i in range(n_hid)])

    mask_in = widen(pattern_in, BLOCK)
    mask_out = widen(pattern_out, BLOCK)
    w_in_eff = w_in * mask_in
    w_out_eff = w_out * mask_out
    w_in_got = partner(w_in_eff)
    w_out_got = partner(w_out_eff)
    placed = pre_act.reshape(far, NEAR, 2, own, width)
    first = (row % (far // runs)) * runs
    mine = lax.dynamic_slice_in_dim(placed, first, runs, 0)
    mine = lax.dynamic_index_in_dim(mine, row // (far // runs), 1, keepdims=False)
    pre_own = lax.dynamic_index_in_dim(mine, core, 1, keepdims=False).reshape(share, width)
    pre_other = lax.dynamic_index_in_dim(mine, other, 1, keepdims=False).reshape(share, width)
    _, slope = gelu_parts(jnp.concatenate([pre_own, partner(pre_other)], axis=1))

    value, _ = gelu_parts(pre_act)
    act = value.astype(jnp.bfloat16).reshape(placed.shape)
    act = act.transpose(2, 1, 0, 3, 4).reshape(2, half, width)

    which = lax.broadcasted_iota(jnp.int32, (far, 2, own, features), 1)
    rows = swap(jnp.where(which == 0, out_grad, inputs), "hid", far_groups)
    rows, w_out_got, w_in_got, slope, w_in_eff, w_out_eff, act = lax.optimization_barrier(
        (rows, w_out_got, w_in_got, slope, w_in_eff, w_out_eff, act)
    )
    in_block = rows[:, 1].reshape(far * own, features)
    rows = rows[:, 0].reshape(1, far * own, features)
    rows = jnp.broadcast_to(rows, (NEAR, far * own, features))
    rows = swap(rows, "hid", near_groups).reshape(half, features)

    n = lax.axis_index("hid") // 2 % NEAR
    steps = [0, 1, NEAR - 1, 2]
    spots = jnp.stack([(n + NEAR - step) % NEAR for step in steps]).astype(jnp.int32)

    def shifted(step):
        step = step - NEAR if step == NEAR - 1 else step
        pairs = [(i, (i + 2 * step) % n_hid) for i in range(n_hid)]
        return lax.ppermute(in_block, "hid", pairs)

    in_blocks = [in_block] + [shifted(step) for step in steps[1:]]

    partial = local(
        act_grad_body,
        struct((half, 2 * width), jnp.bfloat16),
        4 * half * features * width,
        rows,
        w_out_eff,
        w_out_got,
    )
    parts = swap(partial.reshape(n_row, share, 2 * width), "row")
    copies = local(
        delta_body,
        struct((n_row, share, 2 * width), jnp.bfloat16),
        n_row * share * width,
        parts,
        slope,
    )
    delta = swap(copies, "row").reshape(half, 2 * width)

    block = 2 * BLOCK
    back = pl.pallas_call(
        in_grad_body,
        out_shape=struct((half, features), jnp.bfloat16),
        grid=(features // block,),
        in_specs=[pl.BlockSpec((half, 2 * width), lambda i: (0, 0))]
        + [pl.BlockSpec((block, width), lambda i: (i, 0))] * 2,
        out_specs=pl.BlockSpec((half, block), lambda i: (0, i)),
        compiler_params=pltpu.CompilerParams(vmem_limit_bytes=24 * 2**20),
        cost_estimate=pl.CostEstimate(
            flops=4 * half * features * width,
            bytes_accessed=8 * half * features,
            transcendentals=0,
        ),
    )(delta, w_in_eff, w_in_got)
    back = swap(back.reshape(NEAR, far * own, features), "hid", near_groups)
    scale = 1.0 / math.sqrt(tokens)
    delta_got = partner(delta[:, width:])
    w_out_grad = local(
        lambda *refs: w_out_grad_body(scale, *refs),
        struct((width, features), jnp.bfloat16),
        2 * tokens * features * width,
        lax.dynamic_index_in_dim(act, core, 0, keepdims=False),
        lax.dynamic_index_in_dim(act, other, 0, keepdims=False),
        rows,
        partner(rows),
        mask_out,
    )
    back, delta_got, w_out_grad = lax.optimization_barrier((back, delta_got, w_out_grad))
    back = local(sum_body, struct((far * own, features), jnp.bfloat16), back.size, back)
    back = swap(back.reshape(far, own, features), "hid", far_groups)
    in_grad = local(sum_body, struct((own, features), jnp.bfloat16), back.size, back)

    in_rows = pl.pallas_call(
        place_body,
        out_shape=struct((half, features), jnp.bfloat16),
        in_specs=[pl.BlockSpec(memory_space=pltpu.SMEM)]
        + [pl.BlockSpec(memory_space=pltpu.VMEM)] * NEAR,
        out_specs=pl.BlockSpec(memory_space=pltpu.VMEM),
        compiler_params=pltpu.CompilerParams(vmem_limit_bytes=24 * 2**20),
        cost_estimate=pl.CostEstimate(
            flops=0, bytes_accessed=4 * half * features, transcendentals=0
        ),
    )(spots, *in_blocks)

    w_in_grad = local(
        lambda *refs: w_in_grad_body(scale, *refs),
        struct((features, width), jnp.bfloat16),
        2 * tokens * features * width,
        in_rows,
        partner(in_rows),
        delta[:, :width],
        delta_got,
        mask_in,
    )
    return (in_grad, w_in_grad, w_out_grad)


def solution(mesh):
    placed = (
        P("hid", "row"),
        P("hid", "row"),
        P(None, "hid"),
        P("row", "hid"),
        P("hid", "row"),
        P("row", "hid"),
        P("hid", "row"),
    )
    return jax.shard_map(
        lambda *blocks: shards(mesh.shape["hid"], mesh.shape["row"], *blocks),
        mesh=mesh,
        in_specs=placed,
        out_specs=(P("hid", "row"), P("row", "hid"), P("hid", "row")),
        check_vma=False,
    )
```

```python
import math

import jax
import jax.numpy as jnp
from jax import lax
from jax.experimental import pallas as pl
from jax.experimental.pallas import tpu as pltpu
from jax.sharding import PartitionSpec as P

BLOCK = 128
NEAR = 4
CONTRACT_LAST = (((1,), (1,)), ((), ()))
CONTRACT_FIRST = (((0,), (0,)), ((), ()))


def widen(pattern, block):
    rows, cols = pattern.shape
    wide = jnp.broadcast_to(
        pattern.astype(jnp.bfloat16)[:, None, :, None], (rows, block, cols, block)
    )
    return wide.reshape(rows * block, cols * block)


def gelu_parts(pre_act):
    values = pre_act.astype(jnp.float32)
    return jax.jvp(lambda v: jax.nn.gelu(v, approximate=True), (values,), (jnp.ones_like(values),))


def groups(n_hid):
    far = n_hid // 2 // NEAR
    at = lambda k, n, c: 2 * (NEAR * k + n) + c
    return (
        [[at(k, n, c) for k in range(far)] for n in range(NEAR) for c in range(2)],
        [[at(k, n, c) for n in range(NEAR)] for k in range(far) for c in range(2)],
    )


def swap(x, axis, within=None):
    return lax.all_to_all(x, axis, 0, 0, axis_index_groups=within, tiled=True)


def local(body, out_shape, flops, *args):
    size = sum(a.size * a.dtype.itemsize for a in (*args, out_shape))
    return pl.pallas_call(
        body,
        out_shape=out_shape,
        in_specs=[pl.BlockSpec(memory_space=pltpu.VMEM)] * len(args),
        out_specs=pl.BlockSpec(memory_space=pltpu.VMEM),
        compiler_params=pltpu.CompilerParams(vmem_limit_bytes=24 * 2**20),
        cost_estimate=pl.CostEstimate(flops=flops, bytes_accessed=size, transcendentals=0),
    )(*args)


def act_grad_body(rows_ref, own_ref, got_ref, out_ref):
    width = own_ref.shape[0]
    rows = rows_ref[...]
    for place, weight_ref in ((0, own_ref), (width, got_ref)):
        partial = lax.dot_general(
            rows, weight_ref[...], CONTRACT_LAST, preferred_element_type=jnp.float32
        )
        out_ref[:, place : place + width] = partial.astype(out_ref.dtype)


def place_body(spots_ref, *refs):
    *blocks, out_ref = refs
    for block, block_ref in enumerate(blocks):
        count = block_ref.shape[0]
        out_ref[pl.ds(pl.multiple_of(spots_ref[block] * count, count), count), :] = block_ref[...]


def delta_body(parts_ref, slope_ref, out_ref):
    total = parts_ref[0].astype(jnp.float32)
    for part in range(1, parts_ref.shape[0]):
        total = total + parts_ref[part].astype(jnp.float32)
    delta = (total * slope_ref[...]).astype(out_ref.dtype)
    for copy in range(out_ref.shape[0]):
        out_ref[copy] = delta


def in_grad_body(delta_ref, own_ref, got_ref, out_ref):
    width = own_ref.shape[1]
    total = lax.dot_general(
        delta_ref[:, :width], own_ref[...], CONTRACT_LAST, preferred_element_type=jnp.float32
    )
    total = total + lax.dot_general(
        delta_ref[:, width:], got_ref[...], CONTRACT_LAST, preferred_element_type=jnp.float32
    )
    out_ref[...] = total.astype(out_ref.dtype)


def sum_body(parts_ref, out_ref):
    total = parts_ref[0].astype(jnp.float32)
    for part in range(1, parts_ref.shape[0]):
        total = total + parts_ref[part].astype(jnp.float32)
    out_ref[...] = total.astype(out_ref.dtype)


def over_tokens(left, right):
    return lax.dot_general(left, right, CONTRACT_FIRST, preferred_element_type=jnp.float32)


def w_in_grad_body(scale, rows_ref, rows_got_ref, delta_ref, delta_got_ref, mask_ref, out_ref):
    grad = over_tokens(rows_ref[...], delta_ref[...])
    grad = grad + over_tokens(rows_got_ref[...], delta_got_ref[...])
    out_ref[...] = (grad * scale * mask_ref[...].astype(jnp.float32)).astype(out_ref.dtype)


def w_out_grad_body(scale, act_ref, act_other_ref, rows_ref, rows_got_ref, mask_ref, out_ref):
    grad = over_tokens(act_ref[...], rows_ref[...])
    grad = grad + over_tokens(act_other_ref[...], rows_got_ref[...])
    out_ref[...] = (grad * scale * mask_ref[...].astype(jnp.float32)).astype(out_ref.dtype)


def shards(n_hid, n_row, inputs, out_grad, pre_act, w_in, w_out, pattern_in, pattern_out):
    far_groups, near_groups = groups(n_hid)
    far = n_hid // 2 // NEAR
    tokens, width = pre_act.shape
    own, features = out_grad.shape
    half = tokens // 2
    share = half // n_row
    runs = share // own
    core = lax.axis_index("hid") % 2
    row = lax.axis_index("row")
    struct = jax.ShapeDtypeStruct

    other = 1 - core

    def partner(x):
        return lax.ppermute(x, "hid", [(i, i ^ 1) for i in range(n_hid)])

    mask_in = widen(pattern_in, BLOCK)
    mask_out = widen(pattern_out, BLOCK)
    w_in_eff = w_in * mask_in
    w_out_eff = w_out * mask_out
    w_in_got = partner(w_in_eff)
    w_out_got = partner(w_out_eff)
    placed = pre_act.reshape(far, NEAR, 2, own, width)
    first = (row % (far // runs)) * runs
    mine = lax.dynamic_slice_in_dim(placed, first, runs, 0)
    mine = lax.dynamic_index_in_dim(mine, row // (far // runs), 1, keepdims=False)
    pre_own = lax.dynamic_index_in_dim(mine, core, 1, keepdims=False).reshape(share, width)
    pre_other = lax.dynamic_index_in_dim(mine, other, 1, keepdims=False).reshape(share, width)
    _, slope = gelu_parts(jnp.concatenate([pre_own, partner(pre_other)], axis=1))

    value, _ = gelu_parts(pre_act)
    act = value.astype(jnp.bfloat16).reshape(placed.shape)
    act = act.transpose(2, 1, 0, 3, 4).reshape(2, half, width)

    both = jnp.concatenate([out_grad, inputs], axis=1)
    rows = swap(jnp.broadcast_to(both[None], (far, own, 2 * features)), "hid", far_groups)
    rows, w_out_got, w_in_got, slope, w_in_eff, w_out_eff, act = lax.optimization_barrier(
        (rows, w_out_got, w_in_got, slope, w_in_eff, w_out_eff, act)
    )
    rows = rows.reshape(far * own, 2 * features)
    in_block = rows[:, features:]
    rows = jnp.broadcast_to(rows[None, :, :features], (NEAR, far * own, features))
    rows = swap(rows, "hid", near_groups).reshape(half, features)

    n = lax.axis_index("hid") // 2 % NEAR
    steps = [0, 1, NEAR - 1, 2]
    spots = jnp.stack([(n + NEAR - step) % NEAR for step in steps]).astype(jnp.int32)

    def shifted(step):
        ways = {1: (1, 1), NEAR - 1: (-1, -1), 2: (2, 2 - NEAR)}[step]
        pairs = [(i, (i + 2 * ways[i % 2]) % n_hid) for i in range(n_hid)]
        return lax.ppermute(in_block, "hid", pairs)

    in_blocks = [in_block] + [shifted(step) for step in steps[1:]]

    partial = local(
        act_grad_body,
        struct((half, 2 * width), jnp.bfloat16),
        4 * half * features * width,
        rows,
        w_out_eff,
        w_out_got,
    )
    parts = swap(partial.reshape(n_row, share, 2 * width), "row")
    copies = local(
        delta_body,
        struct((n_row, share, 2 * width), jnp.bfloat16),
        n_row * share * width,
        parts,
        slope,
    )
    delta = swap(copies, "row").reshape(half, 2 * width)

    back = local(
        in_grad_body,
        struct((half, features), jnp.bfloat16),
        4 * half * features * width,
        delta,
        w_in_eff,
        w_in_got,
    )
    back = swap(back.reshape(NEAR, far * own, features), "hid", near_groups)
    scale = 1.0 / math.sqrt(tokens)
    delta_got = partner(delta[:, width:])
    w_out_grad = local(
        lambda *refs: w_out_grad_body(scale, *refs),
        struct((width, features), jnp.bfloat16),
        2 * tokens * features * width,
        lax.dynamic_index_in_dim(act, core, 0, keepdims=False),
        lax.dynamic_index_in_dim(act, other, 0, keepdims=False),
        rows,
        partner(rows),
        mask_out,
    )
    back, delta_got, w_out_grad = lax.optimization_barrier((back, delta_got, w_out_grad))
    back = local(sum_body, struct((far * own, features), jnp.bfloat16), back.size, back)
    back = swap(back.reshape(far, own, features), "hid", far_groups)
    in_grad = local(sum_body, struct((own, features), jnp.bfloat16), back.size, back)

    in_rows = pl.pallas_call(
        place_body,
        out_shape=struct((half, features), jnp.bfloat16),
        in_specs=[pl.BlockSpec(memory_space=pltpu.SMEM)]
        + [pl.BlockSpec(memory_space=pltpu.VMEM)] * NEAR,
        out_specs=pl.BlockSpec(memory_space=pltpu.VMEM),
        compiler_params=pltpu.CompilerParams(vmem_limit_bytes=24 * 2**20),
        cost_estimate=pl.CostEstimate(
            flops=0, bytes_accessed=4 * half * features, transcendentals=0
        ),
    )(spots, *in_blocks)

    w_in_grad = local(
        lambda *refs: w_in_grad_body(scale, *refs),
        struct((features, width), jnp.bfloat16),
        2 * tokens * features * width,
        in_rows,
        partner(in_rows),
        delta[:, :width],
        delta_got,
        mask_in,
    )
    return (in_grad, w_in_grad, w_out_grad)


def solution(mesh):
    placed = (
        P("hid", "row"),
        P("hid", "row"),
        P(None, "hid"),
        P("row", "hid"),
        P("hid", "row"),
        P("row", "hid"),
        P("hid", "row"),
    )
    return jax.shard_map(
        lambda *blocks: shards(mesh.shape["hid"], mesh.shape["row"], *blocks),
        mesh=mesh,
        in_specs=placed,
        out_specs=(P("hid", "row"), P("row", "hid"), P("hid", "row")),
        check_vma=False,
    )
```

```python
import math

import jax
import jax.numpy as jnp
from jax import lax
from jax.experimental import pallas as pl
from jax.experimental.pallas import tpu as pltpu
from jax.sharding import PartitionSpec as P

BLOCK = 128
NEAR = 4
CONTRACT_LAST = (((1,), (1,)), ((), ()))
CONTRACT_FIRST = (((0,), (0,)), ((), ()))


def widen(pattern, block):
    rows, cols = pattern.shape
    wide = jnp.broadcast_to(
        pattern.astype(jnp.bfloat16)[:, None, :, None], (rows, block, cols, block)
    )
    return wide.reshape(rows * block, cols * block)


def gelu_parts(pre_act):
    values = pre_act.astype(jnp.float32)
    return jax.jvp(lambda v: jax.nn.gelu(v, approximate=True), (values,), (jnp.ones_like(values),))


def groups(n_hid):
    far = n_hid // 2 // NEAR
    at = lambda k, n, c: 2 * (NEAR * k + n) + c
    return (
        [[at(k, n, c) for k in range(far)] for n in range(NEAR) for c in range(2)],
        [[at(k, n, c) for n in range(NEAR)] for k in range(far) for c in range(2)],
    )


def swap(x, axis, within=None):
    return lax.all_to_all(x, axis, 0, 0, axis_index_groups=within, tiled=True)


def local(body, out_shape, flops, *args):
    size = sum(a.size * a.dtype.itemsize for a in (*args, out_shape))
    return pl.pallas_call(
        body,
        out_shape=out_shape,
        in_specs=[pl.BlockSpec(memory_space=pltpu.VMEM)] * len(args),
        out_specs=pl.BlockSpec(memory_space=pltpu.VMEM),
        compiler_params=pltpu.CompilerParams(vmem_limit_bytes=24 * 2**20),
        cost_estimate=pl.CostEstimate(flops=flops, bytes_accessed=size, transcendentals=0),
    )(*args)


def act_grad_body(rows_ref, own_ref, got_ref, out_ref):
    width = own_ref.shape[0]
    rows = rows_ref[...]
    for place, weight_ref in ((0, own_ref), (width, got_ref)):
        partial = lax.dot_general(
            rows, weight_ref[...], CONTRACT_LAST, preferred_element_type=jnp.float32
        )
        out_ref[:, place : place + width] = partial.astype(out_ref.dtype)


def place_body(spots_ref, *refs):
    *blocks, out_ref = refs
    for block, block_ref in enumerate(blocks):
        count = block_ref.shape[0]
        out_ref[pl.ds(pl.multiple_of(spots_ref[block] * count, count), count), :] = block_ref[...]


def delta_body(parts_ref, slope_ref, out_ref):
    total = parts_ref[0].astype(jnp.float32)
    for part in range(1, parts_ref.shape[0]):
        total = total + parts_ref[part].astype(jnp.float32)
    delta = (total * slope_ref[...]).astype(out_ref.dtype)
    for copy in range(out_ref.shape[0]):
        out_ref[copy] = delta


def in_grad_body(delta_ref, own_ref, got_hbm, out_ref, got_ref, arrived):
    width = own_ref.shape[1]
    load = pltpu.make_async_copy(got_hbm, got_ref, arrived)
    load.start()
    total = lax.dot_general(
        delta_ref[:, :width], own_ref[...], CONTRACT_LAST, preferred_element_type=jnp.float32
    )
    load.wait()
    total = total + lax.dot_general(
        delta_ref[:, width:], got_ref[...], CONTRACT_LAST, preferred_element_type=jnp.float32
    )
    out_ref[...] = total.astype(out_ref.dtype)


def sum_body(parts_ref, out_ref):
    total = parts_ref[0].astype(jnp.float32)
    for part in range(1, parts_ref.shape[0]):
        total = total + parts_ref[part].astype(jnp.float32)
    out_ref[...] = total.astype(out_ref.dtype)


def over_tokens(left, right):
    return lax.dot_general(left, right, CONTRACT_FIRST, preferred_element_type=jnp.float32)


def w_in_grad_body(scale, rows_ref, rows_got_ref, delta_ref, delta_got_ref, mask_ref, out_ref):
    grad = over_tokens(rows_ref[...], delta_ref[...])
    grad = grad + over_tokens(rows_got_ref[...], delta_got_ref[...])
    out_ref[...] = (grad * scale * mask_ref[...].astype(jnp.float32)).astype(out_ref.dtype)


def w_out_grad_body(scale, act_ref, act_other_ref, rows_ref, rows_got_ref, mask_ref, out_ref):
    grad = over_tokens(act_ref[...], rows_ref[...])
    grad = grad + over_tokens(act_other_ref[...], rows_got_ref[...])
    out_ref[...] = (grad * scale * mask_ref[...].astype(jnp.float32)).astype(out_ref.dtype)


def shards(n_hid, n_row, inputs, out_grad, pre_act, w_in, w_out, pattern_in, pattern_out):
    far_groups, near_groups = groups(n_hid)
    far = n_hid // 2 // NEAR
    tokens, width = pre_act.shape
    own, features = out_grad.shape
    half = tokens // 2
    share = half // n_row
    runs = share // own
    core = lax.axis_index("hid") % 2
    row = lax.axis_index("row")
    struct = jax.ShapeDtypeStruct

    other = 1 - core

    def partner(x):
        return lax.ppermute(x, "hid", [(i, i ^ 1) for i in range(n_hid)])

    mask_in = widen(pattern_in, BLOCK)
    mask_out = widen(pattern_out, BLOCK)
    w_in_eff = w_in * mask_in
    w_out_eff = w_out * mask_out
    w_in_got = partner(w_in_eff)
    w_out_got = partner(w_out_eff)
    placed = pre_act.reshape(far, NEAR, 2, own, width)
    first = (row % (far // runs)) * runs
    mine = lax.dynamic_slice_in_dim(placed, first, runs, 0)
    mine = lax.dynamic_index_in_dim(mine, row // (far // runs), 1, keepdims=False)
    pre_own = lax.dynamic_index_in_dim(mine, core, 1, keepdims=False).reshape(share, width)
    pre_other = lax.dynamic_index_in_dim(mine, other, 1, keepdims=False).reshape(share, width)
    _, slope = gelu_parts(jnp.concatenate([pre_own, partner(pre_other)], axis=1))

    value, _ = gelu_parts(pre_act)
    act = value.astype(jnp.bfloat16).reshape(placed.shape)
    act = act.transpose(2, 1, 0, 3, 4).reshape(2, half, width)

    both = jnp.concatenate([out_grad, inputs], axis=1)
    rows = swap(jnp.broadcast_to(both[None], (far, own, 2 * features)), "hid", far_groups)
    rows, w_out_got, w_in_got, slope, w_in_eff, w_out_eff, act = lax.optimization_barrier(
        (rows, w_out_got, w_in_got, slope, w_in_eff, w_out_eff, act)
    )
    rows = rows.reshape(far * own, 2 * features)
    in_block = rows[:, features:]
    rows = jnp.broadcast_to(rows[None, :, :features], (NEAR, far * own, features))
    rows = swap(rows, "hid", near_groups).reshape(half, features)

    n = lax.axis_index("hid") // 2 % NEAR
    steps = [0, 1, NEAR - 1, 2]
    spots = jnp.stack([(n + NEAR - step) % NEAR for step in steps]).astype(jnp.int32)

    def shifted(step):
        step = step - NEAR if step == NEAR - 1 else step
        pairs = [(i, (i + 2 * step) % n_hid) for i in range(n_hid)]
        return lax.ppermute(in_block, "hid", pairs)

    in_blocks = [in_block] + [shifted(step) for step in steps[1:]]

    partial = local(
        act_grad_body,
        struct((half, 2 * width), jnp.bfloat16),
        4 * half * features * width,
        rows,
        w_out_eff,
        w_out_got,
    )
    parts = swap(partial.reshape(n_row, share, 2 * width), "row")
    copies = local(
        delta_body,
        struct((n_row, share, 2 * width), jnp.bfloat16),
        n_row * share * width,
        parts,
        slope,
    )
    delta = swap(copies, "row").reshape(half, 2 * width)

    back = pl.pallas_call(
        in_grad_body,
        out_shape=struct((half, features), jnp.bfloat16),
        in_specs=[pl.BlockSpec(memory_space=pltpu.VMEM)] * 2
        + [pl.BlockSpec(memory_space=pl.ANY)],
        out_specs=pl.BlockSpec(memory_space=pltpu.VMEM),
        scratch_shapes=[pltpu.VMEM((features, width), jnp.bfloat16), pltpu.SemaphoreType.DMA],
        compiler_params=pltpu.CompilerParams(vmem_limit_bytes=24 * 2**20),
        cost_estimate=pl.CostEstimate(
            flops=4 * half * features * width,
            bytes_accessed=8 * half * features,
            transcendentals=0,
        ),
    )(delta, w_in_eff, w_in_got)
    back = swap(back.reshape(NEAR, far * own, features), "hid", near_groups)
    scale = 1.0 / math.sqrt(tokens)
    delta_got = partner(delta[:, width:])
    w_out_grad = local(
        lambda *refs: w_out_grad_body(scale, *refs),
        struct((width, features), jnp.bfloat16),
        2 * tokens * features * width,
        lax.dynamic_index_in_dim(act, core, 0, keepdims=False),
        lax.dynamic_index_in_dim(act, other, 0, keepdims=False),
        rows,
        partner(rows),
        mask_out,
    )
    back, delta_got, w_out_grad = lax.optimization_barrier((back, delta_got, w_out_grad))
    back = local(sum_body, struct((far * own, features), jnp.bfloat16), back.size, back)
    back = swap(back.reshape(far, own, features), "hid", far_groups)
    in_grad = local(sum_body, struct((own, features), jnp.bfloat16), back.size, back)

    in_rows = pl.pallas_call(
        place_body,
        out_shape=struct((half, features), jnp.bfloat16),
        in_specs=[pl.BlockSpec(memory_space=pltpu.SMEM)]
        + [pl.BlockSpec(memory_space=pltpu.VMEM)] * NEAR,
        out_specs=pl.BlockSpec(memory_space=pltpu.VMEM),
        compiler_params=pltpu.CompilerParams(vmem_limit_bytes=24 * 2**20),
        cost_estimate=pl.CostEstimate(
            flops=0, bytes_accessed=4 * half * features, transcendentals=0
        ),
    )(spots, *in_blocks)

    w_in_grad = local(
        lambda *refs: w_in_grad_body(scale, *refs),
        struct((features, width), jnp.bfloat16),
        2 * tokens * features * width,
        in_rows,
        partner(in_rows),
        delta[:, :width],
        delta_got,
        mask_in,
    )
    return (in_grad, w_in_grad, w_out_grad)


def solution(mesh):
    placed = (
        P("hid", "row"),
        P("hid", "row"),
        P(None, "hid"),
        P("row", "hid"),
        P("hid", "row"),
        P("row", "hid"),
        P("hid", "row"),
    )
    return jax.shard_map(
        lambda *blocks: shards(mesh.shape["hid"], mesh.shape["row"], *blocks),
        mesh=mesh,
        in_specs=placed,
        out_specs=(P("hid", "row"), P("row", "hid"), P("hid", "row")),
        check_vma=False,
    )
```
